128 devices in a mesh: section: 16 (over y, z_hi, core), peer: 8 (over x, z_lo).
Axes of the slice: x: 4, y: 4, z: 4 (z_hi: 2, z_lo: 2; z = z_hi * 2 + z_lo), core: 2. Of those that a mesh axis runs over, the one named last changes fastest.
Arguments:
- codes: bfloat16 [32768, 1024], P(('section', 'peer')), may hold values from -6 to 6
- routes: int32 [128, 2], P(('section', 'peer')), may hold values from 0 to 7, as said below
- w_up: bfloat16 [16, 1024, 4096], P('section'), may hold values from -0.1875 to 0.1875
- w_down: bfloat16 [16, 4096, 1024], P('section'), may hold values from -0.09375 to 0.09375
- cotangent: bfloat16 [65536, 1024], P(('section', 'peer')), may hold values from -6 to 6
Outputs:
- next_codes: bfloat16 [65536, 1024], P(('section', 'peer'))
- code_grads: bfloat16 [32768, 1024], P(('section', 'peer'))
- up_grad: bfloat16 [16, 1024, 4096], P('section', 'peer')
- down_grad: bfloat16 [16, 4096, 1024], P('section', 'peer')
The draws below stay inside these ranges and needn't reach their ends.
Inputs may be any that keep to these rules, and one draw needn't show every extreme that they name: `routes`: each sender's 2 blocks go to different peers. In every section every peer receives at least one block and at most 4, and some peer receives exactly 4.
All inputs are finite; a program needn't handle non-finite values.
Results may differ from the reference program's by a relative error of at most 0.019.
Values may be sent and summed in bfloat16 or wider, within the bound.
A program may use at most 256 MiB of HBM per device.

```python
import jax
import jax.numpy as jnp
from jax import lax

B = 1024
D = 4096
BLK = 128
NBLK = 2
LOAD_MAX = 4
SEND_ROWS = 32768
SLOT_ROWS = 65536
N_SECTION = 16
N_PEER = 8


def draw_routes(key, part):
    key = jax.random.fold_in(key, 11)
    ranks = jnp.arange(N_PEER, dtype=jnp.int32)
    first = jnp.where(ranks < LOAD_MAX, 0, ranks - (LOAD_MAX - 1))
    second = ranks % (N_PEER - 1) + 1

    def one_section(section_key):
        key_a, key_b, key_c = jax.random.split(section_key, 3)
        order = jax.random.permutation(key_a, N_PEER).astype(jnp.int32)
        senders = jax.random.permutation(key_b, N_PEER).astype(jnp.int32)
        flips = jax.random.randint(key_c, (N_PEER,), 0, 2)
        left = jnp.where(flips == 1, second, first)
        right = jnp.where(flips == 1, first, second)
        dest = order[jnp.stack([left, right], axis=1)]
        return jnp.zeros((N_PEER, NBLK), jnp.int32).at[senders].set(dest)
    keys = jax.random.split(key, N_SECTION)
    return jax.vmap(one_section)(keys).reshape(N_SECTION * N_PEER, NBLK).astype(jnp.int32)


def level_of(own_key, shape, cuts, low, top_value):
    def one(axis_at, blocks):
        draws = jax.random.uniform(jax.random.fold_in(jax.random.fold_in(own_key, 6), axis_at), (blocks,), jnp.float32, low / len(cuts), top_value / len(cuts))
        return jnp.repeat(jnp.exp(draws), shape[axis_at] // blocks).reshape((-1,) + (1,) * (len(shape) - axis_at - 1))

    loudness = one(*cuts[0])
    for cut in cuts[1:]:
        loudness = loudness * one(*cut)
    return loudness


def bell_draw(stream_key, extent, scale, reach, pieces=(), kind=jnp.bfloat16):
    array = scale * jax.random.normal(stream_key, extent, jnp.float32)
    if pieces:
        array = array * level_of(stream_key, extent, pieces, -0.22, 0.18)
    return jnp.clip(array, -reach, reach).astype(kind)


def setup_inputs(seed: int = 0) -> dict:
    streams_of = jax.random.split(jax.random.key(seed), 6)
    codes = bell_draw(streams_of[0], (SEND_ROWS, B), 1.0, 6.0, ((0, 128),))
    routes = draw_routes(jax.random.fold_in(streams_of[5], 71), 0)
    w_up = bell_draw(streams_of[2], (N_SECTION, B, D), B ** -0.5, 0.1875, ((0, 16),))
    w_down = bell_draw(streams_of[3], (N_SECTION, D, B), D ** -0.5, 0.09375, ((0, 16),))
    cotangent = bell_draw(streams_of[4], (SLOT_ROWS, B), 1.0, 6.0, ((0, 128),))
    return dict(codes=codes, routes=routes, w_up=w_up, w_down=w_down, cotangent=cotangent)


eps = 1e-05

def layer(inputs, up_w, down_w, cot):
    x = jnp.dot(inputs, up_w, preferred_element_type=jnp.float32)
    r = lax.rsqrt(lax.optimization_barrier(jnp.mean(x * x, axis=-1, keepdims=True)) + eps)
    z = x * r
    act = jax.nn.silu(z).astype(jnp.bfloat16)
    y = jnp.dot(act, down_w, preferred_element_type=jnp.float32)
    out = (inputs.astype(jnp.float32) + y).astype(jnp.bfloat16)
    back = lax.dot_general(cot, down_w, (((1,), (1,)), ((), ())), preferred_element_type=jnp.float32)
    sig = jax.nn.sigmoid(z)
    dz = back * sig * (1.0 + z * (1.0 - sig))
    dx = (r * dz - x * (r * r * r) * lax.optimization_barrier(jnp.mean(x * dz, axis=-1, keepdims=True))).astype(jnp.bfloat16)
    in_grad = lax.dot_general(dx, up_w, (((1,), (1,)), ((), ())), preferred_element_type=jnp.float32)
    in_grad = (in_grad + cot.astype(jnp.float32)).astype(jnp.bfloat16)
    return (out, act, dx, in_grad)

def reference(codes, routes, w_up, w_down, cotangent):
    width = codes.shape[1]
    blocks = codes.reshape(N_SECTION, N_PEER * NBLK, BLK * width)
    table = routes.reshape(N_SECTION, N_PEER, NBLK)
    targets = jnp.arange(N_PEER, dtype=jnp.int32)
    slots = jnp.arange(LOAD_MAX, dtype=jnp.int32)

    def plan(tab):
        hit = tab[None, :, :] == targets[:, None, None]
        live = jnp.any(hit, axis=2)
        rank = jnp.cumsum(live.astype(jnp.int32), axis=1) - 1
        sel = live[:, None, :] & (rank[:, None, :] == slots[None, :, None])
        full = sel[:, :, :, None] & hit[:, None, :, :]
        return full.reshape(N_PEER * LOAD_MAX, N_PEER * NBLK).astype(jnp.bfloat16)
    plans = jax.vmap(plan)(table)
    packed = lax.map(lambda pair: jnp.dot(pair[0], pair[1], preferred_element_type=jnp.float32).astype(jnp.bfloat16), (plans, blocks))
    inputs = jnp.roll(packed, 1, axis=0).reshape(N_SECTION, N_PEER * LOAD_MAX * BLK, width)
    cot = cotangent.reshape(N_SECTION, N_PEER * LOAD_MAX * BLK, width)
    factor = 1.0 / (N_PEER * NBLK)

    def section_work(items):
        inp, up_w, down_w, grad_in = items
        out, act, dx, in_grad = layer(inp, up_w, down_w, grad_in)
        up_g = lax.dot_general(inp, dx, (((0,), (0,)), ((), ())), preferred_element_type=jnp.float32)
        down_g = lax.dot_general(act, grad_in, (((0,), (0,)), ((), ())), preferred_element_type=jnp.float32)
        return (out, in_grad, (up_g * factor).astype(jnp.bfloat16), (down_g * factor).astype(jnp.bfloat16))
    outs, in_grads, ups, downs = lax.map(section_work, (inputs, w_up, w_down, cot))
    back = jnp.roll(in_grads.reshape(N_SECTION, N_PEER * LOAD_MAX, BLK * width), -1, axis=0)
    sent = lax.map(lambda pair: lax.dot_general(pair[0], pair[1], (((0,), (0,)), ((), ())), preferred_element_type=jnp.float32).astype(jnp.bfloat16), (plans, back))
    return (outs.reshape(-1, width), sent.reshape(-1, width), ups, downs)
```

```python
import functools

import jax
import jax.numpy as jnp
from jax import lax
from jax.experimental import pallas as pl
from jax.experimental.pallas import tpu as pltpu
from jax.sharding import PartitionSpec as P

eps = 1e-05
MESH = pl.DeviceIdType.MESH
f32 = jnp.float32
bf16 = jnp.bfloat16
ROWS_ROWS = (((0,), (0,)), ((), ()))
COLS_COLS = (((1,), (1,)), ((), ()))


def dot(a, b, dims=(((1,), (0,)), ((), ()))):
    return lax.dot_general(a, b, dims, preferred_element_type=f32)


def gates(x, r):
    z = x * r
    sig = 0.5 * jnp.tanh(0.5 * z) + 0.5
    act = z * sig
    slope = sig * (1.0 + z - act)
    return act, slope


def kernel(
    routes, codes, w_up, w_down, cot,
    out, grads, up_out, down_out,
    wu, wd, codes_all, cot_all, table_v, table_s, plan, live, stats,
    xbuf, x2buf, inp_own, inp3, cot2, yacc, down_acc, up_acc,
    out_v, up_v, down_v, ig_v,
    ssem, rsem, lsem,
):
    peers = lax.axis_size("peer")
    sections = lax.axis_size("section")
    slots = cot_all.shape[1]
    nblk = codes_all.shape[1]
    blk, width = codes_all.shape[2:]
    chunks, _, cols = wu.shape
    model = chunks * cols
    ring = peers // 2
    half = 2 * blk

    sec, me = lax.axis_index("section"), lax.axis_index("peer")
    nxt, prv = lax.rem(sec + 1, sections), lax.rem(sec + sections - 1, sections)
    xi, zi = me // 2, lax.rem(me, 2)
    zo = 1 - zi

    def at(dx, z):
        return 2 * lax.rem(xi + ring + dx, ring) + z

    zp, xr, xl, op = at(0, zo), at(1, zi), at(-1, zi), at(2, zi)
    xrz, xlz, opz = at(1, zo), at(-1, zo), at(2, zo)
    order = (me, zp, xl, xr, xlz, xrz, op, opz)

    barrier = pltpu.get_barrier_semaphore()
    for d in range(1, peers):
        pl.semaphore_signal(
            barrier, inc=1, device_id=(sec, lax.rem(me + d, peers)), device_id_type=MESH
        )
    for s in (nxt, prv):
        pl.semaphore_signal(barrier, inc=1, device_id=(s, me), device_id_type=MESH)

    def local(src, dst, i):
        c = pltpu.make_async_copy(src, dst, lsem.at[i])
        c.start()
        return c

    own_cot = [local(cot.at[pl.ds(k * blk, blk)], cot_all.at[me, k], k) for k in range(slots)]
    load_up = [
        local(w_up.at[:, pl.ds(c * cols, cols)], wu.at[c], slots + c) for c in range(chunks)
    ]
    load_down = [
        local(w_down.at[pl.ds(c * cols, cols)], wd.at[c], slots + chunks + c)
        for c in range(chunks)
    ]
    r0, r1 = routes[0, 0], routes[0, 1]
    lane = lax.broadcasted_iota(jnp.int32, (8, 128), 1)
    table_v[peers] = jnp.where(lane == 0, r0, r1)

    def remote(src, dst, i, s, p):
        return pltpu.make_async_remote_copy(
            src_ref=src, dst_ref=dst, send_sem=ssem.at[i], recv_sem=rsem.at[i],
            device_id=(s, p), device_id_type=MESH,
        )

    sent = []

    def send(src, dst, i, s, p):
        c = remote(src, dst, i, s, p)
        c.start()
        sent.append(c)

    def arrived(dst, i):
        remote(dst, dst, i, sec, zp).wait_recv()

    pieces = nblk + slots
    HOP = 7 * pieces
    ROUTE_HOP = HOP + nblk
    ROUTE = ROUTE_HOP + 1
    STAT = ROUTE + peers
    UPS = STAT + peers
    HOME = UPS + peers

    pl.semaphore_wait(barrier, peers + 1)

    send(table_v.at[peers], table_v.at[me], ROUTE_HOP, nxt, me)
    for b in range(nblk):
        send(codes.at[pl.ds(b * blk, blk)], codes_all.at[me, b], HOP + b, nxt, me)

    def chunk(g, owner):
        if g < nblk:
            return codes_all.at[owner, g]
        return cot_all.at[owner, g - nblk]

    def pass_on(g, owner, o, p):
        send(chunk(g, owner), chunk(g, owner), 7 * g + o - 1, sec, p)

    def start_own(g):
        pass_on(g, me, 1, zp)
        pass_on(g, me, 2, xr)
        pass_on(g, me, 3, xl)

    def wait_for(g, o):
        arrived(chunk(g, order[o]), 7 * g + o - 1)

    def pass_partner(g):
        wait_for(g, 1)
        pass_on(g, zp, 4, xr)
        pass_on(g, zp, 5, xl)

    def pass_opposite(g):
        if g % 2 == 0:
            wait_for(g, 2)
            pass_on(g, xl, 6, xr)
        else:
            wait_for(g, 3)
            pass_on(g, xr, 6, xl)

    def pass_across(g):
        wait_for(g, 6)
        pass_on(g, op, 7, zp)

    code_pieces = range(nblk)
    cot_pieces = range(nblk, pieces)

    for c in own_cot:
        c.wait()
    start_own(nblk)

    arrived(table_v.at[me], ROUTE_HOP)
    for d in range(1, peers):
        send(table_v.at[me], table_v.at[me], ROUTE + d, sec, lax.rem(me + d, peers))
    for g in code_pieces:
        arrived(codes_all.at[me, g], HOP + g)
        start_own(g)

    def codes_rows(j):
        return jnp.concatenate([codes_all[j, b] for b in range(nblk)], axis=0)

    for c in load_up:
        c.wait()

    def x2_step(c, carry):
        x2buf[c] = dot(codes_rows(me), wu[c])
        return carry

    lax.fori_loop(0, chunks // 2, x2_step, 0)
    for g in code_pieces:
        pass_partner(g)
    for g in code_pieces:
        pass_opposite(g)
    for g in list(cot_pieces)[1:]:
        start_own(g)
    lax.fori_loop(chunks // 2, chunks, x2_step, 0)

    for d in range(1, peers):
        j = lax.rem(me + d, peers)
        arrived(table_v.at[j], ROUTE + peers - d)
    fetch = local(table_v, table_s, 0)
    fetch.wait()

    def hits(p, q):
        first, second = table_s[p, 0, 0] == q, table_s[p, 0, 1] == q
        return (
            jnp.where(first | second, 1, 0),
            nblk * p + jnp.where(second, 1, 0),
        )

    def plan_step(q, carry):
        count = 0
        index = [0] * slots
        for p in range(peers):
            hit, block = hits(p, q)
            for k in range(slots):
                index[k] = jnp.where((hit == 1) & (count == k), block, index[k])
            count = count + hit
        for k in range(slots):
            plan[q * slots + k] = index[k]
            live[q * slots + k] = jnp.where(count > k, 1, 0)
        return carry

    lax.fori_loop(0, peers, plan_step, 0)

    def slot_codes(q, k):
        i = plan[q * slots + k]
        rows = codes_all[i // nblk, lax.rem(i, nblk)]
        return jnp.where(live[q * slots + k] == 1, rows, jnp.zeros_like(rows))

    for c in load_down:
        c.wait()
    for g in code_pieces:
        pass_across(g)
    for g in cot_pieces:
        pass_partner(g)
    for g in code_pieces:
        for o in (2, 3, 4, 5, 7):
            if not (o == 2 and g % 2 == 0) and not (o == 3 and g % 2 == 1):
                wait_for(g, o)

    eye = lax.broadcasted_iota(jnp.int32, (blk, blk), 0) == lax.broadcasted_iota(
        jnp.int32, (blk, blk), 1
    )

    def as_row(col):
        return jnp.sum(jnp.where(eye, col, 0.0), axis=0, keepdims=True)

    def as_col(row):
        return jnp.sum(jnp.where(eye, row, 0.0), axis=1, keepdims=True)

    saves = []
    rows_r, rows_c = [], []
    for h in range(slots // 2):
        for j in range(2):
            inp_own[pl.ds(j * blk, blk)] = slot_codes(me, 2 * h + j)

        def x_step(c, ssq):
            x = dot(inp_own[...], wu[c])
            xbuf[c] = x
            return ssq + jnp.sum(x * x, axis=-1, keepdims=True)

        ssq = lax.fori_loop(0, chunks, x_step, jnp.zeros((half, 1), f32))
        r = lax.rsqrt(ssq * (1.0 / model) + eps)
        if h == 0:
            for g in list(cot_pieces)[:2]:
                pass_opposite(g)
        else:
            for g in list(cot_pieces)[:2]:
                pass_across(g)
        yacc[...] = jnp.zeros_like(yacc)
        cot_h = jnp.concatenate([cot_all[me, 2 * h], cot_all[me, 2 * h + 1]], axis=0)

        def y_step(c, m):
            x = xbuf[c]
            act, slope = gates(x, r)
            yacc[...] += dot(act.astype(bf16), wd[c])
            back = dot(cot_h, wd[c], COLS_COLS)
            return m + jnp.sum(x * (back * slope), axis=-1, keepdims=True)

        m = lax.fori_loop(0, chunks, y_step, jnp.zeros((half, 1), f32)) * (1.0 / model)
        if h == 0:
            for g in list(cot_pieces)[2:]:
                pass_opposite(g)
        c3 = (r * r * r) * m
        for j in range(2):
            rows_r.append(as_row(r[j * blk : (j + 1) * blk]))
            rows_c.append(as_row(c3[j * blk : (j + 1) * blk]))
        out_v[pl.ds(h * half, half)] = (inp_own[...].astype(f32) + yacc[...]).astype(bf16)
        saves.append(local(out_v.at[pl.ds(h * half, half)], out.at[pl.ds(h * half, half)], 1 + h))
    stats[me] = jnp.concatenate(rows_r + rows_c, axis=0)
    for d in range(1, peers):
        send(stats.at[me], stats.at[me], STAT + d, sec, lax.rem(me + d, peers))
    for g in list(cot_pieces)[2:]:
        pass_across(g)
    for d in range(1, peers):
        j = lax.rem(me + d, peers)
        arrived(stats.at[j], STAT + peers - d)

    down_acc[...] = jnp.zeros_like(down_acc)
    up_acc[...] = jnp.zeros_like(up_acc)

    def all_slots(q):
        for k in range(slots):
            inp3[pl.ds(k * blk, blk)] = slot_codes(q, k)
        tile = stats[q]
        r = jnp.concatenate([as_col(tile[k : k + 1]) for k in range(slots)], axis=0)
        c3 = jnp.concatenate([as_col(tile[slots + k : slots + k + 1]) for k in range(slots)], axis=0)
        cot_q = jnp.concatenate([cot_all[q, k] for k in range(slots)], axis=0)
        x = dot(inp3[...], wu[me])
        act, slope = gates(x, r)
        down_acc[...] += dot(act.astype(bf16), cot_q, ROWS_ROWS)
        back = dot(cot_q, wd[me], COLS_COLS)
        dx = (r * (back * slope) - x * c3).astype(bf16)
        up_acc[...] += dot(inp3[...], dx, ROWS_ROWS)

    def owner_of(o):
        q = order[0]
        for n in range(1, peers):
            q = jnp.where(o == n, order[n], q)
        return q

    def owner_step(o, carry):
        all_slots(owner_of(o))
        return carry

    lax.fori_loop(0, 2, owner_step, 0)
    for g in cot_pieces:
        for o in (2, 3, 4, 5, 7):
            if not (o == 2 and g % 2 == 0) and not (o == 3 and g % 2 == 1):
                wait_for(g, o)
    lax.fori_loop(2, peers, owner_step, 0)

    factor = 1.0 / (peers * nblk)
    tall = width // peers
    up_v[...] = (up_acc[...] * factor).astype(bf16)
    for d in range(1, peers):
        j = lax.rem(me + d, peers)
        send(
            up_v.at[pl.ds(pl.multiple_of(j * tall, tall), tall)],
            up_out.at[:, pl.ds(pl.multiple_of(me * cols, cols), cols)],
            UPS + d, sec, j,
        )
    saves.append(local(
        up_v.at[pl.ds(pl.multiple_of(me * tall, tall), tall)],
        up_out.at[:, pl.ds(pl.multiple_of(me * cols, cols), cols)], 3,
    ))
    down_v[...] = (down_acc[...] * factor).astype(bf16)
    saves.append(local(down_v, down_out, 4))

    r2, c2 = [], []
    for b in range(nblk):
        q = table_s[me, 0, b]
        k = 0
        for p in range(peers):
            hit, _ = hits(p, q)
            k = k + jnp.where(p < me, hit, 0)
        k = jnp.minimum(k, slots - 1)
        cot2[pl.ds(b * blk, blk)] = cot_all[q, k]
        tile = stats[q]
        sub = lax.broadcasted_iota(jnp.int32, tile.shape, 0)
        r2.append(as_col(jnp.sum(jnp.where(sub == k, tile, 0.0), axis=0, keepdims=True)))
        c2.append(as_col(jnp.sum(jnp.where(sub == slots + k, tile, 0.0), axis=0, keepdims=True)))
    r2, c2 = jnp.concatenate(r2, axis=0), jnp.concatenate(c2, axis=0)
    yacc[...] = cot2[...].astype(f32)

    def home_step(c, carry):
        x = x2buf[c]
        _, slope = gates(x, r2)
        back = dot(cot2[...], wd[c], COLS_COLS)
        dx = (r2 * (back * slope) - x * c2).astype(bf16)
        yacc[...] += dot(dx, wu[c], COLS_COLS)
        return carry

    lax.fori_loop(0, chunks, home_step, 0)
    ig_v[...] = yacc[...].astype(bf16)
    send(ig_v, grads, HOME, prv, me)

    for c in saves:
        c.wait()
    for d in range(1, peers):
        j = lax.rem(me + peers - d, peers)
        arrived(up_out.at[:, pl.ds(pl.multiple_of(j * cols, cols), cols)], UPS + d)
    arrived(grads, HOME)
    for c in sent:
        c.wait_send()


def shards(codes, routes, w_up, w_down, cotangent):
    peers = lax.axis_size("peer")
    nblk = routes.shape[1]
    rows, width = codes.shape
    blk = rows // nblk
    slots = cotangent.shape[0] // blk
    model = w_up.shape[2]
    cols = model // peers
    half = 2 * blk
    anywhere = pl.BlockSpec(memory_space=pl.ANY)
    copies = 7 * (nblk + slots) + nblk + 2 + 3 * peers
    out, grads, up, down = pl.pallas_call(
        kernel,
        out_shape=(
            jax.ShapeDtypeStruct((slots * blk, width), bf16),
            jax.ShapeDtypeStruct((rows, width), bf16),
            jax.ShapeDtypeStruct((width // peers, model), bf16),
            jax.ShapeDtypeStruct((cols, width), bf16),
        ),
        in_specs=[pl.BlockSpec(memory_space=pltpu.SMEM)] + [anywhere] * 4,
        out_specs=[anywhere] * 4,
        scratch_shapes=[
            pltpu.VMEM((peers, width, cols), bf16),
            pltpu.VMEM((peers, cols, width), bf16),
            pltpu.VMEM((peers, nblk, blk, width), bf16),
            pltpu.VMEM((peers, slots, blk, width), bf16),
            pltpu.VMEM((peers + 1, 8, 128), jnp.int32),
            pltpu.SMEM((peers + 1, 8, 128), jnp.int32),
            pltpu.SMEM((peers * slots,), jnp.int32),
            pltpu.SMEM((peers * slots,), jnp.int32),
            pltpu.VMEM((peers, 2 * slots, blk), f32),
            pltpu.VMEM((peers, half, cols), f32),
            pltpu.VMEM((peers, rows, cols), f32),
            pltpu.VMEM((half, width), bf16),
            pltpu.VMEM((slots * blk, width), bf16),
            pltpu.VMEM((rows, width), bf16),
            pltpu.VMEM((half, width), f32),
            pltpu.VMEM((cols, width), f32),
            pltpu.VMEM((width, cols), f32),
            pltpu.VMEM((slots * blk, width), bf16),
            pltpu.VMEM((width, cols), bf16),
            pltpu.VMEM((cols, width), bf16),
            pltpu.VMEM((rows, width), bf16),
            pltpu.SemaphoreType.DMA((copies,)),
            pltpu.SemaphoreType.DMA((copies,)),
            pltpu.SemaphoreType.DMA((slots + 2 * peers,)),
        ],
        compiler_params=pltpu.CompilerParams(
            collective_id=0, has_side_effects=True, vmem_limit_bytes=60 * 1024 * 1024,
        ),
        name="relay",
    )(routes, codes, w_up[0], w_down[0], cotangent)
    return out, grads, up[None], down[None]


def solution(mesh):
    placed = (
        P(("section", "peer"), None),
        P(("section", "peer"), None),
        P("section", None, None),
        P("section", None, None),
        P(("section", "peer"), None),
    )
    return jax.shard_map(
        shards,
        mesh=mesh,
        in_specs=placed,
        out_specs=(
            P(("section", "peer"), None),
            P(("section", "peer"), None),
            P("section", "peer", None),
            P("section", "peer", None),
        ),
        check_vma=False,
    )
```

```python
import functools

import jax
import jax.numpy as jnp
from jax import lax
from jax.experimental import pallas as pl
from jax.experimental.pallas import tpu as pltpu
from jax.sharding import PartitionSpec as P

eps = 1e-05
MESH = pl.DeviceIdType.MESH
f32 = jnp.float32
bf16 = jnp.bfloat16
ROWS_ROWS = (((0,), (0,)), ((), ()))
COLS_COLS = (((1,), (1,)), ((), ()))


def dot(a, b, dims=(((1,), (0,)), ((), ()))):
    return lax.dot_general(a, b, dims, preferred_element_type=f32)


def gates(x, r):
    z = x * r
    sig = 0.5 * jnp.tanh(0.5 * z) + 0.5
    act = z * sig
    slope = sig * (1.0 + z - act)
    return act, slope


def kernel(
    routes, codes, w_up, w_down, cot,
    out, grads, up_out, down_out,
    wu, wd, codes_all, cot_own, cot_all, table_v, table_s, plan, live, base, packed, stats,
    xbuf, x2buf, bbuf, inp_own, inp3, cot3, yacc, move, land,
    out_v, up_v, down_v, ig_v,
    ssem, rsem, lsem,
):
    peers = lax.axis_size("peer")
    sections = lax.axis_size("section")
    slots = cot_own.shape[0]
    nblk = codes_all.shape[1]
    blk, width = codes_all.shape[2:]
    chunks, _, cols = wu.shape
    model = chunks * cols
    ring = peers // 2
    half = 2 * blk
    low, high = pl.ds(0, blk // 2), pl.ds(blk // 2, blk // 2)

    sec, me = lax.axis_index("section"), lax.axis_index("peer")
    nxt, prv = lax.rem(sec + 1, sections), lax.rem(sec + sections - 1, sections)
    xi, zi = me // 2, lax.rem(me, 2)
    zo = 1 - zi

    def at(dx, z):
        return 2 * lax.rem(xi + ring + dx, ring) + z

    zp, xr, xl, op = at(0, zo), at(1, zi), at(-1, zi), at(2, zi)
    xrz, xlz, opz = at(1, zo), at(-1, zo), at(2, zo)
    order = (me, zp, xl, xr, xlz, xrz, op, opz)

    barrier = pltpu.get_barrier_semaphore()
    for d in range(1, peers):
        pl.semaphore_signal(
            barrier, inc=1, device_id=(sec, lax.rem(me + d, peers)), device_id_type=MESH
        )
    for s in (nxt, prv):
        pl.semaphore_signal(barrier, inc=1, device_id=(s, me), device_id_type=MESH)

    def local(src, dst, i):
        c = pltpu.make_async_copy(src, dst, lsem.at[i])
        c.start()
        return c

    load_first = local(cot.at[pl.ds(0, blk)], cot_all.at[0, me], slots)
    load_cot = [local(cot.at[pl.ds(k * blk, blk)], cot_own.at[k], k) for k in range(slots)]
    load_up = [
        local(w_up.at[:, pl.ds(c * cols, cols)], wu.at[c], slots + 1 + c) for c in range(chunks)
    ]
    load_down = [
        local(w_down.at[pl.ds(c * cols, cols)], wd.at[c], slots + 1 + chunks + c)
        for c in range(chunks)
    ]
    r0, r1 = routes[0, 0], routes[0, 1]
    lane = lax.broadcasted_iota(jnp.int32, (8, 128), 1)
    table_v[peers] = jnp.where(lane == 0, r0, r1)

    def remote(src, dst, i, s, p):
        return pltpu.make_async_remote_copy(
            src_ref=src, dst_ref=dst, send_sem=ssem.at[i], recv_sem=rsem.at[i],
            device_id=(s, p), device_id_type=MESH,
        )

    sent = []

    def send(src, dst, i, s, p):
        c = remote(src, dst, i, s, p)
        c.start()
        sent.append(c)

    def arrived(dst, i):
        remote(dst, dst, i, sec, zp).wait_recv()

    FIRST, MORE = nblk, nblk + 1
    pieces = nblk + 2
    HOP = 7 * pieces
    ROUTE_HOP = HOP + nblk
    ROUTE = ROUTE_HOP + 1
    STAT = ROUTE + peers
    UPS = STAT + peers
    HOME = UPS + peers
    PACK = HOME + 1

    pl.semaphore_wait(barrier, peers + 1)

    send(table_v.at[peers], table_v.at[me], ROUTE_HOP, nxt, me)
    for b in range(nblk):
        send(codes.at[pl.ds(b * blk, blk)], codes_all.at[me, b], HOP + b, nxt, me)

    def chunk(g, owner):
        if g < nblk:
            return codes_all.at[owner, g]
        return cot_all.at[g - nblk, owner]

    def pass_on(g, owner, o, p):
        send(chunk(g, owner), chunk(g, owner), 7 * g + o - 1, sec, p)

    def start_own(g):
        pass_on(g, me, 1, zp)
        pass_on(g, me, 2, xr)
        pass_on(g, me, 3, xl)

    def wait_for(g, o):
        arrived(chunk(g, order[o]), 7 * g + o - 1)

    def pass_partner(g):
        wait_for(g, 1)
        pass_on(g, zp, 4, xr)
        pass_on(g, zp, 5, xl)

    def pass_opposite(g):
        if g % 2 == 0:
            wait_for(g, 2)
            pass_on(g, xl, 6, xr)
        else:
            wait_for(g, 3)
            pass_on(g, xr, 6, xl)

    def pass_across(g):
        wait_for(g, 6)
        pass_on(g, op, 7, zp)

    def wait_rest(g):
        for o in (3 if g % 2 == 0 else 2, 4, 5, 7):
            wait_for(g, o)

    load_first.wait()
    start_own(FIRST)

    arrived(table_v.at[me], ROUTE_HOP)
    for d in range(1, peers):
        send(table_v.at[me], table_v.at[me], ROUTE + d, sec, lax.rem(me + d, peers))
    for g in range(nblk):
        arrived(codes_all.at[me, g], HOP + g)
        start_own(g)

    for d in range(1, peers):
        j = lax.rem(me + d, peers)
        arrived(table_v.at[j], ROUTE + peers - d)
    fetch = local(table_v, table_s, slots)
    fetch.wait()

    def hits(p, q):
        first, second = table_s[p, 0, 0] == q, table_s[p, 0, 1] == q
        return (
            jnp.where(first | second, 1, 0),
            nblk * p + jnp.where(second, 1, 0),
        )

    def plan_step(q, before):
        count = 0
        index = [0] * slots
        for p in range(peers):
            hit, block = hits(p, q)
            for k in range(slots):
                index[k] = jnp.where((hit == 1) & (count == k), block, index[k])
            count = count + hit
        for k in range(slots):
            plan[q * slots + k] = index[k]
            live[q * slots + k] = jnp.where(count > k, 1, 0)
        base[q] = before
        return before + count - 1

    lax.fori_loop(0, peers, plan_step, 0)

    def packed_at(q, k):
        return jnp.where(live[q * slots + k] == 1, base[q] + k - 1, -1)

    for c in load_cot:
        c.wait()

    def mine(j):
        rows = jnp.zeros((blk, width), bf16)
        for k in range(1, slots):
            rows = jnp.where(packed_at(me, k) == j, cot_own[k], rows)
        return rows

    move[0] = mine(opz)
    send(move.at[0], land.at[0], PACK + 0, sec, zp)
    move[5] = mine(xrz)
    send(move.at[5], land.at[5], PACK + 5, sec, xr)
    move[6] = mine(xlz)
    send(move.at[6], land.at[6], PACK + 6, sec, xl)

    def codes_rows(j):
        return jnp.concatenate([codes_all[j, b] for b in range(nblk)], axis=0)

    for c in load_up:
        c.wait()

    def x2_step(c, carry):
        x2buf[c] = dot(codes_rows(me), wu[c])
        return carry

    lax.fori_loop(0, chunks // 2, x2_step, 0)
    for g in range(nblk):
        pass_partner(g)
    arrived(land.at[0], PACK + 0)
    move[1] = mine(op) + land[0]
    send(move.at[1, low], land.at[1, low], PACK + 1, sec, xr)
    send(move.at[1, high], land.at[1, high], PACK + 2, sec, xl)
    for g in range(nblk):
        pass_opposite(g)
    lax.fori_loop(chunks // 2, chunks, x2_step, 0)
    arrived(land.at[1, low], PACK + 1)
    arrived(land.at[1, high], PACK + 2)
    move[3] = mine(xr)
    move[3, low] = move[3, low] + land[1, low]
    send(move.at[3], land.at[3], PACK + 3, sec, xr)
    move[4] = mine(xl)
    move[4, high] = move[4, high] + land[1, high]
    send(move.at[4], land.at[4], PACK + 4, sec, xl)
    arrived(land.at[5], PACK + 5)
    arrived(land.at[6], PACK + 6)
    move[2] = mine(zp) + land[5] + land[6]
    send(move.at[2], land.at[2], PACK + 7, sec, zp)
    pass_partner(FIRST)

    for c in load_down:
        c.wait()

    def back_step(c, carry):
        rows = jnp.concatenate([cot_own[k] for k in range(slots)], axis=0)
        bbuf[c] = dot(rows, wd[c], COLS_COLS)
        return carry

    lax.fori_loop(0, chunks // 2, back_step, 0)
    for g in range(nblk):
        pass_across(g)
    arrived(land.at[3], PACK + 3)
    arrived(land.at[4], PACK + 4)
    arrived(land.at[2], PACK + 7)
    cot_all[1, me] = mine(me) + land[3] + land[4] + land[2]
    start_own(MORE)
    pass_opposite(FIRST)
    lax.fori_loop(chunks // 2, chunks, back_step, 0)
    for g in range(nblk):
        wait_rest(g)

    eye = lax.broadcasted_iota(jnp.int32, (blk, blk), 0) == lax.broadcasted_iota(
        jnp.int32, (blk, blk), 1
    )

    def as_row(col):
        return jnp.sum(jnp.where(eye, col, 0.0), axis=0, keepdims=True)

    def as_col(row):
        return jnp.sum(jnp.where(eye, row, 0.0), axis=1, keepdims=True)

    def block_codes(i):
        return codes_all[i // nblk, lax.rem(i, nblk)]

    def slot_codes(q, k):
        rows = block_codes(plan[q * slots + k])
        return jnp.where(live[q * slots + k] == 1, rows, jnp.zeros_like(rows))

    saves = []
    rows_r, rows_c = [], []
    for h in range(slots // 2):
        for j in range(2):
            inp_own[pl.ds(j * blk, blk)] = slot_codes(me, 2 * h + j)

        def x_step(c, ssq):
            x = dot(inp_own[...], wu[c])
            xbuf[c] = x
            return ssq + jnp.sum(x * x, axis=-1, keepdims=True)

        ssq = lax.fori_loop(0, chunks, x_step, jnp.zeros((half, 1), f32))
        r = lax.rsqrt(ssq * (1.0 / model) + eps)
        if h == 0:
            pass_partner(MORE)
            pass_across(FIRST)
        else:
            pass_across(MORE)
        yacc[...] = jnp.zeros_like(yacc)

        def y_step(c, m):
            x = xbuf[c]
            act, slope = gates(x, r)
            yacc[...] += dot(act.astype(bf16), wd[c])
            back = bbuf[c, pl.ds(h * half, half)]
            return m + jnp.sum(x * (back * slope), axis=-1, keepdims=True)

        m = lax.fori_loop(0, chunks, y_step, jnp.zeros((half, 1), f32)) * (1.0 / model)
        if h == 0:
            pass_opposite(MORE)
        c3 = (r * r * r) * m
        for j in range(2):
            rows_r.append(as_row(r[j * blk : (j + 1) * blk]))
            rows_c.append(as_row(c3[j * blk : (j + 1) * blk]))
        out_v[pl.ds(h * half, half)] = (inp_own[...].astype(f32) + yacc[...]).astype(bf16)
        saves.append(local(out_v.at[pl.ds(h * half, half)], out.at[pl.ds(h * half, half)], h))
    stats[me] = jnp.concatenate(rows_r + rows_c, axis=0)
    for d in range(1, peers):
        send(stats.at[me], stats.at[me], STAT + d, sec, lax.rem(me + d, peers))

    def packed_step(j, carry):
        block, peer, slot = 0, 0, 1
        for q in range(peers):
            for k in range(1, slots):
                hit = packed_at(q, k) == j
                block = jnp.where(hit, plan[q * slots + k], block)
                peer = jnp.where(hit, q, peer)
                slot = jnp.where(hit, k, slot)
        packed[3 * j], packed[3 * j + 1], packed[3 * j + 2] = block, peer, slot
        return carry

    lax.fori_loop(0, peers, packed_step, 0)
    wait_rest(FIRST)
    for d in range(1, peers):
        j = lax.rem(me + d, peers)
        arrived(stats.at[j], STAT + peers - d)

    def row_values(q, k):
        tile = stats[q]
        sub = lax.broadcasted_iota(jnp.int32, tile.shape, 0)
        return [
            as_col(jnp.sum(jnp.where(sub == n, tile, 0.0), axis=0, keepdims=True))
            for n in (k, slots + k)
        ]

    parts = width // cols
    sums = pl.ds(0, cols)
    for n in range(2 * parts):
        bbuf[n, sums] = jnp.zeros((cols, cols), f32)

    def four(blocks):
        rs, cs = [], []
        for n, (rows, cots, q, k) in enumerate(blocks):
            inp3[pl.ds(n * blk, blk)] = rows
            cot3[pl.ds(n * blk, blk)] = cots
            r, c3 = row_values(q, k)
            rs.append(r)
            cs.append(c3)
        r, c3 = jnp.concatenate(rs, axis=0), jnp.concatenate(cs, axis=0)
        x = dot(inp3[...], wu[me])
        act, slope = gates(x, r)
        act = act.astype(bf16)
        back = dot(cot3[...], wd[me], COLS_COLS)
        dx = (r * (back * slope) - x * c3).astype(bf16)
        for n in range(parts):
            bbuf[n, sums] += dot(inp3[:, pl.ds(n * cols, cols)], dx, ROWS_ROWS)
            bbuf[parts + n, sums] += dot(act, cot3[:, pl.ds(n * cols, cols)], ROWS_ROWS)

    def first_step(i, carry):
        blocks = []
        for n in range(4):
            q = 4 * i + n
            blocks.append((block_codes(plan[q * slots]), cot_all[0, q], q, 0))
        four(blocks)
        return carry

    def more_step(i, carry):
        blocks = []
        for n in range(4):
            j = 4 * i + n
            block, q, k = packed[3 * j], packed[3 * j + 1], packed[3 * j + 2]
            blocks.append((block_codes(block), cot_all[1, j], q, k))
        four(blocks)
        return carry

    lax.fori_loop(0, peers // 4, first_step, 0)
    wait_rest(MORE)
    lax.fori_loop(0, peers // 4, more_step, 0)

    factor = 1.0 / (peers * nblk)
    tall = width // peers
    for n in range(parts):
        up_v[pl.ds(n * cols, cols)] = (bbuf[n, sums] * factor).astype(bf16)
    for d in range(1, peers):
        j = lax.rem(me + d, peers)
        send(
            up_v.at[pl.ds(pl.multiple_of(j * tall, tall), tall)],
            up_out.at[:, pl.ds(pl.multiple_of(me * cols, cols), cols)],
            UPS + d, sec, j,
        )
    saves.append(local(
        up_v.at[pl.ds(pl.multiple_of(me * tall, tall), tall)],
        up_out.at[:, pl.ds(pl.multiple_of(me * cols, cols), cols)], 2,
    ))
    for n in range(parts):
        down_v[:, pl.ds(n * cols, cols)] = (bbuf[parts + n, sums] * factor).astype(bf16)
    saves.append(local(down_v, down_out, 3))

    r2, c2 = [], []
    for b in range(nblk):
        q = table_s[me, 0, b]
        k = 0
        for p in range(peers):
            hit, _ = hits(p, q)
            k = k + jnp.where(p < me, hit, 0)
        k = jnp.minimum(k, slots - 1)
        j = jnp.clip(base[q] + k - 1, 0, peers - 1)
        cot3[pl.ds(b * blk, blk)] = jnp.where(k == 0, cot_all[0, q], cot_all[1, j])
        r, c3 = row_values(q, k)
        r2.append(r)
        c2.append(c3)
    r2, c2 = jnp.concatenate(r2, axis=0), jnp.concatenate(c2, axis=0)
    two = pl.ds(0, nblk * blk)
    yacc[...] = cot3[two].astype(f32)

    def home_step(c, carry):
        x = x2buf[c]
        _, slope = gates(x, r2)
        back = dot(cot3[two], wd[c], COLS_COLS)
        dx = (r2 * (back * slope) - x * c2).astype(bf16)
        yacc[...] += dot(dx, wu[c], COLS_COLS)
        return carry

    lax.fori_loop(0, chunks, home_step, 0)
    ig_v[...] = yacc[...].astype(bf16)
    send(ig_v, grads, HOME, prv, me)

    for c in saves:
        c.wait()
    for d in range(1, peers):
        j = lax.rem(me + peers - d, peers)
        arrived(up_out.at[:, pl.ds(pl.multiple_of(j * cols, cols), cols)], UPS + d)
    arrived(grads, HOME)
    for c in sent:
        c.wait_send()


def copy_kernel(*refs):
    n = (len(refs) - 2) // 3
    sources, results, held = refs[:n], refs[n : 2 * n], refs[2 * n : 3 * n]
    in_sem, out_sem = refs[3 * n :]
    loads = []
    for src, mid in zip(sources, held):
        rows = src.shape[0] // 4
        for k in range(4):
            part = pl.ds(k * rows, rows)
            loads.append(pltpu.make_async_copy(src.at[part], mid.at[part], in_sem.at[len(loads)]))
    for c in loads:
        c.start()
    stores = []
    for mid, dst in zip(held, results):
        rows = dst.shape[0] // 4
        for k in range(4):
            part = pl.ds(k * rows, rows)
            loads[len(stores)].wait()
            c = pltpu.make_async_copy(mid.at[part], dst.at[part], out_sem.at[len(stores)])
            c.start()
            stores.append(c)
    for c in stores:
        c.wait()


def shards(codes, routes, w_up, w_down, cotangent):
    peers = lax.axis_size("peer")
    nblk = routes.shape[1]
    rows, width = codes.shape
    blk = rows // nblk
    slots = cotangent.shape[0] // blk
    model = w_up.shape[2]
    cols = model // peers
    half = 2 * blk
    anywhere = pl.BlockSpec(memory_space=pl.ANY)
    copies = 7 * (nblk + 2) + nblk + 2 + 3 * peers + 8
    shapes = (
        jax.ShapeDtypeStruct((slots * blk, width), bf16),
        jax.ShapeDtypeStruct((rows, width), bf16),
        jax.ShapeDtypeStruct((width // peers, model), bf16),
        jax.ShapeDtypeStruct((cols, width), bf16),
    )
    results = pl.pallas_call(
        kernel,
        out_shape=shapes,
        in_specs=[pl.BlockSpec(memory_space=pltpu.SMEM)] + [anywhere] * 4,
        out_specs=[anywhere] * 4,
        scratch_shapes=[
            pltpu.VMEM((peers, width, cols), bf16),
            pltpu.VMEM((peers, cols, width), bf16),
            pltpu.VMEM((peers, nblk, blk, width), bf16),
            pltpu.VMEM((slots, blk, width), bf16),
            pltpu.VMEM((2, peers, blk, width), bf16),
            pltpu.VMEM((peers + 1, 8, 128), jnp.int32),
            pltpu.SMEM((peers + 1, 8, 128), jnp.int32),
            pltpu.SMEM((peers * slots,), jnp.int32),
            pltpu.SMEM((peers * slots,), jnp.int32),
            pltpu.SMEM((peers,), jnp.int32),
            pltpu.SMEM((3 * peers,), jnp.int32),
            pltpu.VMEM((peers, 2 * slots, blk), f32),
            pltpu.VMEM((peers, half, cols), f32),
            pltpu.VMEM((peers, rows, cols), f32),
            pltpu.VMEM((peers, slots * blk, cols), f32),
            pltpu.VMEM((half, width), bf16),
            pltpu.VMEM((slots * blk, width), bf16),
            pltpu.VMEM((slots * blk, width), bf16),
            pltpu.VMEM((half, width), f32),
            pltpu.VMEM((7, blk, width), bf16),
            pltpu.VMEM((7, blk, width), bf16),
            pltpu.VMEM((slots * blk, width), bf16),
            pltpu.VMEM((width, cols), bf16),
            pltpu.VMEM((cols, width), bf16),
            pltpu.VMEM((rows, width), bf16),
            pltpu.SemaphoreType.DMA((copies,)),
            pltpu.SemaphoreType.DMA((copies,)),
            pltpu.SemaphoreType.DMA((slots + 1 + 2 * peers,)),
        ],
        compiler_params=pltpu.CompilerParams(
            collective_id=0, has_side_effects=True, vmem_limit_bytes=60 * 1024 * 1024,
        ),
        name="relay",
    )(routes, codes, w_up[0], w_down[0], cotangent)
    out, grads, up, down = pl.pallas_call(
        copy_kernel,
        out_shape=shapes,
        in_specs=[anywhere] * 4,
        out_specs=[anywhere] * 4,
        scratch_shapes=[pltpu.VMEM(a.shape, a.dtype) for a in shapes]
        + [pltpu.SemaphoreType.DMA((16,))] * 2,
        name="results",
    )(*results)
    return out, grads, up[None], down[None]


def solution(mesh):
    placed = (
        P(("section", "peer"), None),
        P(("section", "peer"), None),
        P("section", None, None),
        P("section", None, None),
        P(("section", "peer"), None),
    )
    return jax.shard_map(
        shards,
        mesh=mesh,
        in_specs=placed,
        out_specs=(
            P(("section", "peer"), None),
            P(("section", "peer"), None),
            P("section", "peer", None),
            P("section", "peer", None),
        ),
        check_vma=False,
    )
```

```python
import functools

import jax
import jax.numpy as jnp
from jax import lax
from jax.experimental import pallas as pl
from jax.experimental.pallas import tpu as pltpu
from jax.sharding import PartitionSpec as P

eps = 1e-05
MESH = pl.DeviceIdType.MESH
f32 = jnp.float32
bf16 = jnp.bfloat16
ROWS_ROWS = (((0,), (0,)), ((), ()))
COLS_COLS = (((1,), (1,)), ((), ()))


def dot(a, b, dims=(((1,), (0,)), ((), ()))):
    return lax.dot_general(a, b, dims, preferred_element_type=f32)


def gates(x, r):
    z = x * r
    sig = 0.5 * jnp.tanh(0.5 * z) + 0.5
    act = z * sig
    slope = sig * (1.0 + z - act)
    return act, slope


def kernel(
    routes, codes, w_up, w_down, cot,
    out, grads, up_out, down_out,
    wu, wd, codes_all, cot_own, cot_all, table_v, table_s, place, stats,
    xbuf, up_acc, down_acc, inp3, cot3, yacc, move, land,
    up_v, down_v, ig_v, home_v,
    ssem, rsem, lsem,
):
    peers = lax.axis_size("peer")
    sections = lax.axis_size("section")
    slots = cot_own.shape[0]
    nblk = codes_all.shape[1]
    blk, width = codes_all.shape[2:]
    chunks, _, cols = wu.shape
    model = chunks * cols
    ring = peers // 2
    low, high = pl.ds(0, blk // 2), pl.ds(blk // 2, blk // 2)

    sec, me = lax.axis_index("section"), lax.axis_index("peer")
    nxt, prv = lax.rem(sec + 1, sections), lax.rem(sec + sections - 1, sections)
    xi, zi = me // 2, lax.rem(me, 2)
    zo = 1 - zi

    def at(dx, z):
        return 2 * lax.rem(xi + ring + dx, ring) + z

    zp, xr, xl, op = at(0, zo), at(1, zi), at(-1, zi), at(2, zi)
    xrz, xlz, opz = at(1, zo), at(-1, zo), at(2, zo)
    order = (me, zp, xl, xr, xlz, xrz, op, opz)

    barrier = pltpu.get_barrier_semaphore()
    for d in range(1, peers):
        pl.semaphore_signal(
            barrier, inc=1, device_id=(sec, lax.rem(me + d, peers)), device_id_type=MESH
        )
    for s in (nxt, prv):
        pl.semaphore_signal(barrier, inc=1, device_id=(s, me), device_id_type=MESH)

    def local(src, dst, i):
        c = pltpu.make_async_copy(src, dst, lsem.at[i])
        c.start()
        return c

    load_first = local(cot.at[pl.ds(0, blk)], cot_all.at[0, me], slots)
    load_cot = [local(cot.at[pl.ds(k * blk, blk)], cot_own.at[k], k) for k in range(slots)]
    load_up = [
        local(w_up.at[:, pl.ds(c * cols, cols)], wu.at[c], slots + 1 + c) for c in range(chunks)
    ]
    load_down = [
        local(w_down.at[pl.ds(c * cols, cols)], wd.at[c], slots + 1 + chunks + c)
        for c in range(chunks)
    ]
    r0, r1 = routes[0, 0], routes[0, 1]
    lane = lax.broadcasted_iota(jnp.int32, (8, 128), 1)
    table_v[peers] = jnp.where(lane == 0, r0, r1)

    def remote(src, dst, i, s, p):
        return pltpu.make_async_remote_copy(
            src_ref=src, dst_ref=dst, send_sem=ssem.at[i], recv_sem=rsem.at[i],
            device_id=(s, p), device_id_type=MESH,
        )

    sent = []

    def send(src, dst, i, s, p):
        c = remote(src, dst, i, s, p)
        c.start()
        sent.append(c)

    def arrived(dst, i):
        remote(dst, dst, i, sec, zp).wait_recv()

    FIRST, MORE = nblk, nblk + 1
    pieces = nblk + 2
    HOP = 7 * pieces
    ROUTE_HOP = HOP + nblk
    ROUTE = ROUTE_HOP + 1
    STAT = ROUTE + peers
    UPS = STAT + peers
    HOME = UPS + peers
    PACK = HOME + 1

    pl.semaphore_wait(barrier, peers + 1)

    def chunk(g, owner):
        if g < nblk:
            return codes_all.at[owner, g]
        return cot_all.at[g - nblk, owner]

    def pass_on(g, owner, o, p):
        send(chunk(g, owner), chunk(g, owner), 7 * g + o - 1, sec, p)

    def start_across(g):
        pass_on(g, me, 1, zp)

    def start_along(g):
        pass_on(g, me, 2, xr)
        pass_on(g, me, 3, xl)

    def wait_for(g, *numbers):
        for o in numbers:
            arrived(chunk(g, order[o]), 7 * g + o - 1)

    def pass_partner(g):
        wait_for(g, 1)
        pass_on(g, zp, 4, xr)
        pass_on(g, zp, 5, xl)

    def pass_opposite(g):
        if g % 2 == 0:
            wait_for(g, 2)
            pass_on(g, xl, 6, xr)
        else:
            wait_for(g, 3)
            pass_on(g, xr, 6, xl)

    def pass_across(g):
        wait_for(g, 6)
        pass_on(g, op, 7, zp)

    send(table_v.at[peers], table_v.at[me], ROUTE_HOP, nxt, me)
    for b in range(nblk):
        send(codes.at[pl.ds(b * blk, blk)], codes_all.at[me, b], HOP + b, nxt, me)
    load_first.wait()
    start_along(FIRST)
    arrived(table_v.at[me], ROUTE_HOP)
    for d in range(1, peers):
        send(table_v.at[me], table_v.at[me], ROUTE + d, sec, lax.rem(me + d, peers))

    for d in range(1, peers):
        j = lax.rem(me + d, peers)
        arrived(table_v.at[j], ROUTE + peers - d)
    fetch = local(table_v, table_s, slots)
    fetch.wait()

    counts = [0] * peers
    slot_block, slot_live = [0] * slots, [0] * slots
    targets = []
    for p in range(peers):
        for b in range(nblk):
            q = table_s[p, 0, b]
            k = 0
            for n in range(peers):
                k = jnp.where(q == n, counts[n], k)
                counts[n] = counts[n] + jnp.where(q == n, 1, 0)
            for n in range(slots):
                here = (q == me) & (k == n)
                slot_block[n] = jnp.where(here, nblk * p + b, slot_block[n])
                slot_live[n] = jnp.where(here, 1, slot_live[n])
            targets.append((q, k))
    before = [0]
    for n in range(peers - 1):
        before.append(before[n] + counts[n] - 1)
    own_before = 0
    for n in range(peers):
        own_before = jnp.where(me == n, before[n], own_before)
    for n, (q, k) in enumerate(targets):
        ahead = 0
        for m in range(peers):
            ahead = jnp.where(q == m, before[m], ahead)
        place[n] = jnp.clip(jnp.where(k == 0, q, peers + ahead + k - 1), 0, 2 * peers - 1)

    for c in load_cot:
        c.wait()

    def mine(j):
        rows = jnp.zeros((blk, width), bf16)
        for k in range(1, slots):
            hit = (slot_live[k] == 1) & (own_before + k - 1 == j)
            rows = jnp.where(hit, cot_own[k], rows)
        return rows

    move[0] = mine(opz)
    send(move.at[0], land.at[0], PACK + 0, sec, zp)
    move[5] = mine(xrz)
    send(move.at[5], land.at[5], PACK + 5, sec, xr)
    move[6] = mine(xlz)
    send(move.at[6], land.at[6], PACK + 6, sec, xl)
    arrived(codes_all.at[me, 0], HOP)
    start_along(0)
    start_across(0)
    arrived(land.at[0], PACK + 0)
    move[1] = mine(op) + land[0]
    send(move.at[1, low], land.at[1, low], PACK + 1, sec, xr)
    send(move.at[1, high], land.at[1, high], PACK + 2, sec, xl)
    for b in range(1, nblk):
        arrived(codes_all.at[me, b], HOP + b)
        start_along(b)

    two = nblk * blk
    xs, ds = pl.ds(0, two), pl.ds(two, two)

    for c in load_up:
        c.wait()

    def x2_step(c, ssq):
        rows = jnp.concatenate([codes_all[me, b] for b in range(nblk)], axis=0)
        x = dot(rows, wu[c])
        xbuf[c, xs] = x
        return ssq + jnp.sum(x * x, axis=-1, keepdims=True)

    ssq = lax.fori_loop(0, chunks, x2_step, jnp.zeros((two, 1), f32))
    r2 = lax.rsqrt(ssq * (1.0 / model) + eps)

    arrived(land.at[1, low], PACK + 1)
    arrived(land.at[1, high], PACK + 2)
    move[3] = mine(xr)
    move[3, low] = move[3, low] + land[1, low]
    send(move.at[3], land.at[3], PACK + 3, sec, xr)
    move[4] = mine(xl)
    move[4, high] = move[4, high] + land[1, high]
    send(move.at[4], land.at[4], PACK + 4, sec, xl)
    arrived(land.at[5], PACK + 5)
    arrived(land.at[6], PACK + 6)
    move[2] = mine(zp) + land[5] + land[6]
    send(move.at[2], land.at[2], PACK + 7, sec, zp)
    start_across(FIRST)
    pass_opposite(FIRST)
    for b in range(1, nblk):
        start_across(b)

    def slope_step(c, carry):
        xbuf[c, ds] = gates(xbuf[c, xs], r2)[1]
        return carry

    lax.fori_loop(0, chunks, slope_step, 0)

    arrived(land.at[3], PACK + 3)
    arrived(land.at[4], PACK + 4)
    arrived(land.at[2], PACK + 7)
    cot_all[1, me] = mine(me) + land[3] + land[4] + land[2]
    start_along(MORE)
    start_across(MORE)
    pass_partner(FIRST)
    pass_across(FIRST)
    pass_opposite(MORE)
    pass_partner(MORE)
    for g in range(nblk):
        pass_opposite(g)
    pass_partner(0)
    pass_across(MORE)
    for g in range(1, nblk):
        pass_partner(g)

    eye = lax.broadcasted_iota(jnp.int32, (blk, blk), 0) == lax.broadcasted_iota(
        jnp.int32, (blk, blk), 1
    )

    def as_row(col):
        return jnp.sum(jnp.where(eye, col, 0.0), axis=0, keepdims=True)

    def as_col(row):
        return jnp.sum(jnp.where(eye, row, 0.0), axis=1, keepdims=True)

    def cot_block(n):
        i = place[n]
        return cot_all[i // peers, lax.rem(i, peers)]

    for c in load_down:
        c.wait()
    wait_for(FIRST, 3, 4, 5, 7)
    wait_for(MORE, 2, 4, 5, 7)
    for b in range(nblk):
        cot3[pl.ds(b * blk, blk)] = cot_block(nblk * me + b)

    def dz_step(c, m):
        dz = xbuf[c, ds] * dot(cot3[xs], wd[c], COLS_COLS)
        xbuf[c, ds] = dz
        return m + jnp.sum(xbuf[c, xs] * dz, axis=-1, keepdims=True)

    m2 = lax.fori_loop(0, chunks, dz_step, jnp.zeros((two, 1), f32)) * (1.0 / model)
    c2 = (r2 * r2 * r2) * m2
    rows = [as_row(v[b * blk : (b + 1) * blk]) for v in (r2, c2) for b in range(nblk)]
    stats[me] = jnp.concatenate(rows + [jnp.zeros((8 - 2 * nblk, blk), f32)], axis=0)
    for d in range(1, peers):
        send(stats.at[me], stats.at[me], STAT + d, sec, lax.rem(me + d, peers))
    for g in range(nblk):
        pass_across(g)

    yacc[xs] = cot3[xs].astype(f32)

    def home_step(c, carry):
        dx = (r2 * xbuf[c, ds] - xbuf[c, xs] * c2).astype(bf16)
        yacc[xs] += dot(dx, wu[c], COLS_COLS)
        return carry

    lax.fori_loop(0, chunks, home_step, 0)
    ig_v[...] = yacc[xs].astype(bf16)
    send(ig_v, home_v, HOME, prv, me)
    for d in range(1, peers):
        j = lax.rem(me + d, peers)
        arrived(stats.at[j], STAT + peers - d)

    up_acc[...] = jnp.zeros_like(up_acc)
    down_acc[...] = jnp.zeros_like(down_acc)

    def owner_of(o):
        q = order[0]
        for n in range(1, peers):
            q = jnp.where(o == n, order[n], q)
        return q

    def pair_step(i, carry):
        rs, cs = [], []
        for n in range(2):
            p = owner_of(2 * i + n)
            for b in range(nblk):
                part = pl.ds((nblk * n + b) * blk, blk)
                inp3[part] = codes_all[p, b]
                cot3[part] = cot_block(nblk * p + b)
            tile = stats[p]
            rs += [as_col(tile[b : b + 1]) for b in range(nblk)]
            cs += [as_col(tile[nblk + b : nblk + b + 1]) for b in range(nblk)]
        r, c3 = jnp.concatenate(rs, axis=0), jnp.concatenate(cs, axis=0)
        x = dot(inp3[...], wu[me])
        act, slope = gates(x, r)
        act = act.astype(bf16)
        back = dot(cot3[...], wd[me], COLS_COLS)
        dx = (r * (back * slope) - x * c3).astype(bf16)
        up_acc[...] += dot(inp3[...], dx, ROWS_ROWS)
        down_acc[...] += dot(act, cot3[...], ROWS_ROWS)
        return carry

    for g in range(nblk):
        wait_for(g, 3 if g % 2 == 0 else 2)
    lax.fori_loop(0, 2, pair_step, 0)
    for g in range(nblk):
        wait_for(g, 4, 5)
    lax.fori_loop(2, 3, pair_step, 0)
    for g in range(nblk):
        wait_for(g, 7)
    lax.fori_loop(3, peers // 2, pair_step, 0)

    saves = []
    factor = 1.0 / (peers * nblk)
    tall = width // peers
    up_v[...] = (up_acc[...] * factor).astype(bf16)
    for d in range(1, peers):
        j = lax.rem(me + d, peers)
        send(
            up_v.at[pl.ds(pl.multiple_of(j * tall, tall), tall)],
            up_out.at[:, pl.ds(pl.multiple_of(me * cols, cols), cols)],
            UPS + d, sec, j,
        )
    saves.append(local(
        up_v.at[pl.ds(pl.multiple_of(me * tall, tall), tall)],
        up_out.at[:, pl.ds(pl.multiple_of(me * cols, cols), cols)], 0,
    ))
    down_v[...] = (down_acc[...] * factor).astype(bf16)
    saves.append(local(down_v, down_out, 1))

    for k in range(slots):
        rows = codes_all[slot_block[k] // nblk, lax.rem(slot_block[k], nblk)]
        inp3[pl.ds(k * blk, blk)] = jnp.where(slot_live[k] == 1, rows, jnp.zeros_like(rows))

    def x_step(c, ssq):
        x = dot(inp3[...], wu[c])
        xbuf[c] = x
        return ssq + jnp.sum(x * x, axis=-1, keepdims=True)

    ssq = lax.fori_loop(0, chunks, x_step, jnp.zeros((slots * blk, 1), f32))
    r = lax.rsqrt(ssq * (1.0 / model) + eps)
    arrived(home_v, HOME)
    saves.append(local(home_v, grads, 2))
    yacc[...] = inp3[...].astype(f32)

    def y_step(c, carry):
        act, _ = gates(xbuf[c], r)
        yacc[...] += dot(act.astype(bf16), wd[c])
        return carry

    lax.fori_loop(0, chunks, y_step, 0)
    cot3[...] = yacc[...].astype(bf16)
    saves.append(local(cot3, out, 3))

    for d in range(1, peers):
        j = lax.rem(me + peers - d, peers)
        arrived(up_out.at[:, pl.ds(pl.multiple_of(j * cols, cols), cols)], UPS + d)
    for c in saves:
        c.wait()
    for c in sent:
        c.wait_send()


def copy_kernel(*refs):
    n = (len(refs) - 2) // 3
    sources, results, held = refs[:n], refs[n : 2 * n], refs[2 * n : 3 * n]
    in_sem, out_sem = refs[3 * n :]
    loads = []
    for src, mid in zip(sources, held):
        rows = src.shape[0] // 4
        for k in range(4):
            part = pl.ds(k * rows, rows)
            loads.append(pltpu.make_async_copy(src.at[part], mid.at[part], in_sem.at[len(loads)]))
    for c in loads:
        c.start()
    stores = []
    for mid, dst in zip(held, results):
        rows = dst.shape[0] // 4
        for k in range(4):
            part = pl.ds(k * rows, rows)
            loads[len(stores)].wait()
            c = pltpu.make_async_copy(mid.at[part], dst.at[part], out_sem.at[len(stores)])
            c.start()
            stores.append(c)
    for c in stores:
        c.wait()


def shards(codes, routes, w_up, w_down, cotangent):
    peers = lax.axis_size("peer")
    nblk = routes.shape[1]
    rows, width = codes.shape
    blk = rows // nblk
    slots = cotangent.shape[0] // blk
    model = w_up.shape[2]
    cols = model // peers
    anywhere = pl.BlockSpec(memory_space=pl.ANY)
    copies = 7 * (nblk + 2) + nblk + 2 + 3 * peers + 8
    shapes = (
        jax.ShapeDtypeStruct((slots * blk, width), bf16),
        jax.ShapeDtypeStruct((rows, width), bf16),
        jax.ShapeDtypeStruct((width // peers, model), bf16),
        jax.ShapeDtypeStruct((cols, width), bf16),
    )
    results = pl.pallas_call(
        kernel,
        out_shape=shapes,
        in_specs=[pl.BlockSpec(memory_space=pltpu.SMEM)] + [anywhere] * 4,
        out_specs=[anywhere] * 4,
        scratch_shapes=[
            pltpu.VMEM((peers, width, cols), bf16),
            pltpu.VMEM((peers, cols, width), bf16),
            pltpu.VMEM((peers, nblk, blk, width), bf16),
            pltpu.VMEM((slots, blk, width), bf16),
            pltpu.VMEM((2, peers, blk, width), bf16),
            pltpu.VMEM((peers + 1, 8, 128), jnp.int32),
            pltpu.SMEM((peers + 1, 8, 128), jnp.int32),
            pltpu.SMEM((2 * peers,), jnp.int32),
            pltpu.VMEM((peers, 8, blk), f32),
            pltpu.VMEM((peers, slots * blk, cols), f32),
            pltpu.VMEM((width, cols), f32),
            pltpu.VMEM((cols, width), f32),
            pltpu.VMEM((slots * blk, width), bf16),
            pltpu.VMEM((slots * blk, width), bf16),
            pltpu.VMEM((slots * blk, width), f32),
            pltpu.VMEM((7, blk, width), bf16),
            pltpu.VMEM((7, blk, width), bf16),
            pltpu.VMEM((width, cols), bf16),
            pltpu.VMEM((cols, width), bf16),
            pltpu.VMEM((rows, width), bf16),
            pltpu.VMEM((rows, width), bf16),
            pltpu.SemaphoreType.DMA((copies,)),
            pltpu.SemaphoreType.DMA((copies,)),
            pltpu.SemaphoreType.DMA((slots + 1 + 2 * peers,)),
        ],
        compiler_params=pltpu.CompilerParams(
            collective_id=0, has_side_effects=True, vmem_limit_bytes=62 * 1024 * 1024,
        ),
        name="relay",
    )(routes, codes, w_up[0], w_down[0], cotangent)
    out, grads, up, down = pl.pallas_call(
        copy_kernel,
        out_shape=shapes,
        in_specs=[anywhere] * 4,
        out_specs=[anywhere] * 4,
        scratch_shapes=[pltpu.VMEM(a.shape, a.dtype) for a in shapes]
        + [pltpu.SemaphoreType.DMA((16,))] * 2,
        name="results",
    )(*results)
    return out, grads, up[None], down[None]


def solution(mesh):
    placed = (
        P(("section", "peer"), None),
        P(("section", "peer"), None),
        P("section", None, None),
        P("section", None, None),
        P(("section", "peer"), None),
    )
    return jax.shard_map(
        shards,
        mesh=mesh,
        in_specs=placed,
        out_specs=(
            P(("section", "peer"), None),
            P(("section", "peer"), None),
            P("section", "peer", None),
            P("section", "peer", None),
        ),
        check_vma=False,
    )
```

```python
import functools

import jax
import jax.numpy as jnp
from jax import lax
from jax.experimental import pallas as pl
from jax.experimental.pallas import tpu as pltpu
from jax.sharding import PartitionSpec as P

eps = 1e-05
MESH = pl.DeviceIdType.MESH
f32 = jnp.float32
bf16 = jnp.bfloat16
ROWS_ROWS = (((0,), (0,)), ((), ()))
COLS_COLS = (((1,), (1,)), ((), ()))


def dot(a, b, dims=(((1,), (0,)), ((), ()))):
    return lax.dot_general(a, b, dims, preferred_element_type=f32)


def gates(x, r):
    z = x * r
    sig = 0.5 * jnp.tanh(0.5 * z) + 0.5
    act = z * sig
    slope = sig * (1.0 + z - act)
    return act, slope


def kernel(
    routes, codes, w_up, w_down, cot,
    out, grads, up_out, down_out,
    wu, wd, codes_all, cot_own, cot_all, table_v, table_s, place, stats,
    xbuf, up_acc, down_acc, inp3, cot3, yacc, move, land,
    up_v, down_v, ig_v, home_v,
    ssem, rsem, lsem,
):
    peers = lax.axis_size("peer")
    sections = lax.axis_size("section")
    slots = cot_own.shape[0]
    nblk = codes_all.shape[1]
    blk, width = codes_all.shape[2:]
    chunks, _, cols = wu.shape
    model = chunks * cols
    ring = peers // 2
    low, high = pl.ds(0, blk // 2), pl.ds(blk // 2, blk // 2)

    sec, me = lax.axis_index("section"), lax.axis_index("peer")
    nxt, prv = lax.rem(sec + 1, sections), lax.rem(sec + sections - 1, sections)
    xi, zi = me // 2, lax.rem(me, 2)
    zo = 1 - zi

    def at(dx, z):
        return 2 * lax.rem(xi + ring + dx, ring) + z

    zp, xr, xl, op = at(0, zo), at(1, zi), at(-1, zi), at(2, zi)
    xrz, xlz, opz = at(1, zo), at(-1, zo), at(2, zo)
    cross_out = lax.rem(sec, 2)
    cross_in = 1 - cross_out

    def crossed(p, cross):
        return p + cross * (1 - 2 * (p % 2 if isinstance(p, int) else lax.rem(p, 2)))

    there, sender = crossed(me, cross_out), crossed(me, cross_in)
    order = (me, zp, xl, xr, xlz, xrz, op, opz)

    barrier = pltpu.get_barrier_semaphore()
    for d in range(1, peers):
        pl.semaphore_signal(
            barrier, inc=1, device_id=(sec, lax.rem(me + d, peers)), device_id_type=MESH
        )
    for s in (nxt, prv):
        for p in range(peers):
            pl.semaphore_signal(barrier, inc=1, device_id=(s, p), device_id_type=MESH)

    def local(src, dst, i):
        c = pltpu.make_async_copy(src, dst, lsem.at[i])
        c.start()
        return c

    load_codes = local(codes, ig_v, slots + 1 + 2 * chunks)
    load_first = local(cot.at[pl.ds(0, blk)], cot_all.at[0, me], slots)
    load_cot = [local(cot.at[pl.ds(k * blk, blk)], cot_own.at[k], k) for k in range(slots)]
    load_up = [
        local(w_up.at[:, pl.ds(c * cols, cols)], wu.at[c], slots + 1 + c) for c in range(chunks)
    ]
    load_down = [
        local(w_down.at[pl.ds(c * cols, cols)], wd.at[c], slots + 1 + chunks + c)
        for c in range(chunks)
    ]
    r0, r1 = routes[0, 0], routes[0, 1]
    lane = lax.broadcasted_iota(jnp.int32, (8, 128), 1)
    table_v[peers] = jnp.where(lane == 0, r0, r1)

    def remote(src, dst, i, s, p):
        return pltpu.make_async_remote_copy(
            src_ref=src, dst_ref=dst, send_sem=ssem.at[i], recv_sem=rsem.at[i],
            device_id=(s, p), device_id_type=MESH,
        )

    sent = []

    def send(src, dst, i, s, p):
        c = remote(src, dst, i, s, p)
        c.start()
        sent.append(c)

    def arrived(dst, i):
        remote(dst, dst, i, sec, zp).wait_recv()

    FIRST, MORE = nblk, nblk + 1
    pieces = nblk + 2
    HOP = 7 * pieces
    ROUTE = HOP + nblk
    STAT = ROUTE + peers
    UPS = STAT + peers
    HOME = UPS + peers
    PACK = HOME + 1

    pl.semaphore_wait(barrier, 3 * peers - 1)

    def chunk(g, owner):
        if g < nblk:
            return codes_all.at[owner, g]
        return cot_all.at[g - nblk, owner]

    def pass_on(g, owner, o, p):
        send(chunk(g, owner), chunk(g, owner), 7 * g + o - 1, sec, p)

    def start_across(g):
        pass_on(g, me, 1, zp)

    def start_along(g):
        pass_on(g, me, 2, xr)
        pass_on(g, me, 3, xl)

    def wait_for(g, *numbers):
        for o in numbers:
            arrived(chunk(g, order[o]), 7 * g + o - 1)

    def pass_partner(g):
        wait_for(g, 1)
        pass_on(g, zp, 4, xr)
        pass_on(g, zp, 5, xl)

    def pass_opposite(g):
        if g % 2 == 0:
            wait_for(g, 2)
            pass_on(g, xl, 6, xr)
        else:
            wait_for(g, 3)
            pass_on(g, xr, 6, xl)

    def pass_across(g):
        wait_for(g, 6)
        pass_on(g, op, 7, zp)

    for d in range(peers):
        send(table_v.at[peers], table_v.at[me], ROUTE + d, nxt, lax.rem(me + d, peers))
    load_codes.wait()
    for b in range(nblk):
        send(ig_v.at[pl.ds(b * blk, blk)], codes_all.at[there, b], HOP + b, nxt, there)
    codes_sent = sent[-nblk:]
    del sent[-nblk:]
    load_first.wait()
    start_along(FIRST)

    for d in range(peers):
        j = lax.rem(me + d, peers)
        arrived(table_v.at[j], ROUTE + (peers - d) % peers)
    fetch = local(table_v, table_s, slots)
    fetch.wait()

    counts = [0] * peers
    slot_block, slot_live = [0] * slots, [0] * slots
    targets = []
    for p in range(peers):
        for b in range(nblk):
            q = table_s[p, 0, b]
            k = 0
            for n in range(peers):
                k = jnp.where(q == n, counts[n], k)
                counts[n] = counts[n] + jnp.where(q == n, 1, 0)
            for n in range(slots):
                here = (q == me) & (k == n)
                slot_block[n] = jnp.where(here, nblk * crossed(p, cross_in) + b, slot_block[n])
                slot_live[n] = jnp.where(here, 1, slot_live[n])
            targets.append((q, k))
    before = [0]
    for n in range(peers - 1):
        before.append(before[n] + counts[n] - 1)
    own_before = 0
    for n in range(peers):
        own_before = jnp.where(me == n, before[n], own_before)
    for n, (q, k) in enumerate(targets):
        ahead = 0
        for m in range(peers):
            ahead = jnp.where(q == m, before[m], ahead)
        place[n] = jnp.clip(jnp.where(k == 0, q, peers + ahead + k - 1), 0, 2 * peers - 1)

    for c in load_cot:
        c.wait()

    def mine(j):
        rows = jnp.zeros((blk, width), bf16)
        for k in range(1, slots):
            hit = (slot_live[k] == 1) & (own_before + k - 1 == j)
            rows = jnp.where(hit, cot_own[k], rows)
        return rows

    def pack_start():
        move[0] = mine(opz)
        send(move.at[0], land.at[0], PACK + 0, sec, zp)
        move[5] = mine(xrz)
        send(move.at[5], land.at[5], PACK + 5, sec, xr)
        move[6] = mine(xlz)
        send(move.at[6], land.at[6], PACK + 6, sec, xl)

    def pack_far():
        arrived(land.at[0], PACK + 0)
        move[1] = mine(op) + land[0]
        send(move.at[1, low], land.at[1, low], PACK + 1, sec, xr)
        send(move.at[1, high], land.at[1, high], PACK + 2, sec, xl)

    def pack_along():
        arrived(land.at[1, low], PACK + 1)
        arrived(land.at[1, high], PACK + 2)
        move[3] = mine(xr)
        move[3, low] = move[3, low] + land[1, low]
        send(move.at[3], land.at[3], PACK + 3, sec, xr)
        move[4] = mine(xl)
        move[4, high] = move[4, high] + land[1, high]
        send(move.at[4], land.at[4], PACK + 4, sec, xl)

    def pack_across():
        arrived(land.at[5], PACK + 5)
        arrived(land.at[6], PACK + 6)
        move[2] = mine(zp) + land[5] + land[6]
        send(move.at[2], land.at[2], PACK + 7, sec, zp)

    def pack_end():
        arrived(land.at[3], PACK + 3)
        arrived(land.at[4], PACK + 4)
        arrived(land.at[2], PACK + 7)
        cot_all[1, me] = mine(me) + land[3] + land[4] + land[2]

    def codes_here(g):
        arrived(codes_all.at[me, g], HOP + g)

    two = nblk * blk
    xs, ds = pl.ds(0, two), pl.ds(two, two)

    def x2_step(c, ssq):
        rows = jnp.concatenate([codes_all[me, b] for b in range(nblk)], axis=0)
        x = dot(rows, wu[c])
        xbuf[c, xs] = x
        return ssq + jnp.sum(x * x, axis=-1, keepdims=True)

    def slope_step(c, r):
        xbuf[c, ds] = gates(xbuf[c, xs], r)[1]
        return r

    pack_start()
    codes_here(0)
    start_along(0)
    start_across(0)
    pack_far()
    codes_here(1)
    start_along(1)
    for c in load_up:
        c.wait()
    ssq = lax.fori_loop(0, chunks, x2_step, jnp.zeros((two, 1), f32))
    r2 = lax.rsqrt(ssq * (1.0 / model) + eps)
    pack_along()
    pack_across()
    start_across(FIRST)
    pass_opposite(FIRST)
    start_across(1)
    lax.fori_loop(0, chunks, slope_step, r2)
    pack_end()
    start_along(MORE)
    start_across(MORE)
    pass_partner(FIRST)
    pass_across(FIRST)
    pass_opposite(MORE)
    pass_partner(MORE)
    pass_opposite(0)
    pass_opposite(1)
    pass_partner(0)
    pass_across(MORE)

    eye = lax.broadcasted_iota(jnp.int32, (blk, blk), 0) == lax.broadcasted_iota(
        jnp.int32, (blk, blk), 1
    )

    def as_row(col):
        return jnp.sum(jnp.where(eye, col, 0.0), axis=0, keepdims=True)

    def as_col(row):
        return jnp.sum(jnp.where(eye, row, 0.0), axis=1, keepdims=True)

    def cot_block(n):
        i = place[n]
        return cot_all[i // peers, lax.rem(i, peers)]

    for c in load_down:
        c.wait()
    wait_for(FIRST, 3, 4, 5, 7)
    wait_for(MORE, 2, 4, 5, 7)
    for b in range(nblk):
        cot3[pl.ds(b * blk, blk)] = cot_block(nblk * sender + b)

    def dz_step(c, m):
        dz = xbuf[c, ds] * dot(cot3[xs], wd[c], COLS_COLS)
        xbuf[c, ds] = dz
        return m + jnp.sum(xbuf[c, xs] * dz, axis=-1, keepdims=True)

    m2 = lax.fori_loop(0, chunks, dz_step, jnp.zeros((two, 1), f32)) * (1.0 / model)
    c2 = (r2 * r2 * r2) * m2
    rows = [as_row(v[b * blk : (b + 1) * blk]) for v in (r2, c2) for b in range(nblk)]
    stats[me] = jnp.concatenate(rows + [jnp.zeros((8 - 2 * nblk, blk), f32)], axis=0)
    for d in range(1, peers):
        send(stats.at[me], stats.at[me], STAT + d, sec, lax.rem(me + d, peers))
    pass_partner(1)
    for g in range(nblk):
        pass_across(g)

    yacc[xs] = cot3[xs].astype(f32)

    def home_step(c, carry):
        dx = (r2 * xbuf[c, ds] - xbuf[c, xs] * c2).astype(bf16)
        yacc[xs] += dot(dx, wu[c], COLS_COLS)
        return carry

    lax.fori_loop(0, chunks, home_step, 0)
    for c in codes_sent:
        c.wait_send()
    ig_v[...] = yacc[xs].astype(bf16)
    send(ig_v, home_v, HOME, prv, sender)
    for d in range(1, peers):
        j = lax.rem(me + d, peers)
        arrived(stats.at[j], STAT + peers - d)

    up_acc[...] = jnp.zeros_like(up_acc)
    down_acc[...] = jnp.zeros_like(down_acc)

    def owner_of(o):
        q = order[0]
        for n in range(1, peers):
            q = jnp.where(o == n, order[n], q)
        return q

    def pair_step(i, carry):
        rs, cs = [], []
        for n in range(2):
            p = owner_of(2 * i + n)
            for b in range(nblk):
                part = pl.ds((nblk * n + b) * blk, blk)
                inp3[part] = codes_all[p, b]
                cot3[part] = cot_block(nblk * crossed(p, cross_in) + b)
            tile = stats[p]
            rs += [as_col(tile[b : b + 1]) for b in range(nblk)]
            cs += [as_col(tile[nblk + b : nblk + b + 1]) for b in range(nblk)]
        r, c3 = jnp.concatenate(rs, axis=0), jnp.concatenate(cs, axis=0)
        x = dot(inp3[...], wu[me])
        act, slope = gates(x, r)
        act = act.astype(bf16)
        back = dot(cot3[...], wd[me], COLS_COLS)
        dx = (r * (back * slope) - x * c3).astype(bf16)
        up_acc[...] += dot(inp3[...], dx, ROWS_ROWS)
        down_acc[...] += dot(act, cot3[...], ROWS_ROWS)
        return carry

    for g in range(nblk):
        wait_for(g, 3 if g % 2 == 0 else 2)
    lax.fori_loop(0, 2, pair_step, 0)
    for g in range(nblk):
        wait_for(g, 4, 5)
    lax.fori_loop(2, 3, pair_step, 0)
    for g in range(nblk):
        wait_for(g, 7)
    lax.fori_loop(3, peers // 2, pair_step, 0)

    saves = []
    factor = 1.0 / (peers * nblk)
    tall = width // peers
    up_v[...] = (up_acc[...] * factor).astype(bf16)
    for j in reversed(order[1:]):
        d = lax.rem(j + peers - me, peers)
        send(
            up_v.at[pl.ds(pl.multiple_of(j * tall, tall), tall)],
            up_out.at[:, pl.ds(pl.multiple_of(me * cols, cols), cols)],
            UPS + d, sec, j,
        )
    saves.append(local(
        up_v.at[pl.ds(pl.multiple_of(me * tall, tall), tall)],
        up_out.at[:, pl.ds(pl.multiple_of(me * cols, cols), cols)], 0,
    ))
    down_v[...] = (down_acc[...] * factor).astype(bf16)
    saves.append(local(down_v, down_out, 1))

    for k in range(slots):
        rows = codes_all[slot_block[k] // nblk, lax.rem(slot_block[k], nblk)]
        inp3[pl.ds(k * blk, blk)] = jnp.where(slot_live[k] == 1, rows, jnp.zeros_like(rows))

    def x_step(c, ssq):
        x = dot(inp3[...], wu[c])
        xbuf[c] = x
        return ssq + jnp.sum(x * x, axis=-1, keepdims=True)

    ssq = lax.fori_loop(0, chunks, x_step, jnp.zeros((slots * blk, 1), f32))
    r = lax.rsqrt(ssq * (1.0 / model) + eps)
    arrived(home_v, HOME)
    saves.append(local(home_v, grads, 2))
    yacc[...] = inp3[...].astype(f32)

    def y_step(c, carry):
        act, _ = gates(xbuf[c], r)
        yacc[...] += dot(act.astype(bf16), wd[c])
        return carry

    lax.fori_loop(0, chunks, y_step, 0)
    cot3[...] = yacc[...].astype(bf16)
    saves.append(local(cot3, out, 3))

    for d in range(1, peers):
        j = lax.rem(me + peers - d, peers)
        arrived(up_out.at[:, pl.ds(pl.multiple_of(j * cols, cols), cols)], UPS + d)
    for c in saves:
        c.wait()
    for c in sent:
        c.wait_send()


def copy_kernel(*refs):
    n = (len(refs) - 2) // 3
    sources, results, held = refs[:n], refs[n : 2 * n], refs[2 * n : 3 * n]
    in_sem, out_sem = refs[3 * n :]
    loads = []
    for src, mid in zip(sources, held):
        rows = src.shape[0] // 4
        for k in range(4):
            part = pl.ds(k * rows, rows)
            loads.append(pltpu.make_async_copy(src.at[part], mid.at[part], in_sem.at[len(loads)]))
    for c in loads:
        c.start()
    stores = []
    for mid, dst in zip(held, results):
        rows = dst.shape[0] // 4
        for k in range(4):
            part = pl.ds(k * rows, rows)
            loads[len(stores)].wait()
            c = pltpu.make_async_copy(mid.at[part], dst.at[part], out_sem.at[len(stores)])
            c.start()
            stores.append(c)
    for c in stores:
        c.wait()


def shards(codes, routes, w_up, w_down, cotangent):
    peers = lax.axis_size("peer")
    nblk = routes.shape[1]
    rows, width = codes.shape
    blk = rows // nblk
    slots = cotangent.shape[0] // blk
    model = w_up.shape[2]
    cols = model // peers
    anywhere = pl.BlockSpec(memory_space=pl.ANY)
    copies = 7 * (nblk + 2) + nblk + 2 + 3 * peers + 8
    shapes = (
        jax.ShapeDtypeStruct((slots * blk, width), bf16),
        jax.ShapeDtypeStruct((rows, width), bf16),
        jax.ShapeDtypeStruct((width // peers, model), bf16),
        jax.ShapeDtypeStruct((cols, width), bf16),
    )
    results = pl.pallas_call(
        kernel,
        out_shape=shapes,
        in_specs=[pl.BlockSpec(memory_space=pltpu.SMEM)] + [anywhere] * 4,
        out_specs=[anywhere] * 4,
        scratch_shapes=[
            pltpu.VMEM((peers, width, cols), bf16),
            pltpu.VMEM((peers, cols, width), bf16),
            pltpu.VMEM((peers, nblk, blk, width), bf16),
            pltpu.VMEM((slots, blk, width), bf16),
            pltpu.VMEM((2, peers, blk, width), bf16),
            pltpu.VMEM((peers + 1, 8, 128), jnp.int32),
            pltpu.SMEM((peers + 1, 8, 128), jnp.int32),
            pltpu.SMEM((2 * peers,), jnp.int32),
            pltpu.VMEM((peers, 8, blk), f32),
            pltpu.VMEM((peers, slots * blk, cols), f32),
            pltpu.VMEM((width, cols), f32),
            pltpu.VMEM((cols, width), f32),
            pltpu.VMEM((slots * blk, width), bf16),
            pltpu.VMEM((slots * blk, width), bf16),
            pltpu.VMEM((slots * blk, width), f32),
            pltpu.VMEM((7, blk, width), bf16),
            pltpu.VMEM((7, blk, width), bf16),
            pltpu.VMEM((width, cols), bf16),
            pltpu.VMEM((cols, width), bf16),
            pltpu.VMEM((rows, width), bf16),
            pltpu.VMEM((rows, width), bf16),
            pltpu.SemaphoreType.DMA((copies,)),
            pltpu.SemaphoreType.DMA((copies,)),
            pltpu.SemaphoreType.DMA((slots + 2 + 2 * peers,)),
        ],
        compiler_params=pltpu.CompilerParams(
            collective_id=0, has_side_effects=True, vmem_limit_bytes=62 * 1024 * 1024,
        ),
        name="relay",
    )(routes, codes, w_up[0], w_down[0], cotangent)
    out, grads, up, down = pl.pallas_call(
        copy_kernel,
        out_shape=shapes,
        in_specs=[anywhere] * 4,
        out_specs=[anywhere] * 4,
        scratch_shapes=[pltpu.VMEM(a.shape, a.dtype) for a in shapes]
        + [pltpu.SemaphoreType.DMA((16,))] * 2,
        name="results",
    )(*results)
    return out, grads, up[None], down[None]


def solution(mesh):
    placed = (
        P(("section", "peer"), None),
        P(("section", "peer"), None),
        P("section", None, None),
        P("section", None, None),
        P(("section", "peer"), None),
    )
    return jax.shard_map(
        shards,
        mesh=mesh,
        in_specs=placed,
        out_specs=(
            P(("section", "peer"), None),
            P(("section", "peer"), None),
            P("section", "peer", None),
            P("section", "peer", None),
        ),
        check_vma=False,
    )
```

```python
import functools

import jax
import jax.numpy as jnp
from jax import lax
from jax.experimental import pallas as pl
from jax.experimental.pallas import tpu as pltpu
from jax.sharding import PartitionSpec as P

eps = 1e-05
MESH = pl.DeviceIdType.MESH
f32 = jnp.float32
bf16 = jnp.bfloat16
ROWS_ROWS = (((0,), (0,)), ((), ()))
COLS_COLS = (((1,), (1,)), ((), ()))


def dot(a, b, dims=(((1,), (0,)), ((), ()))):
    return lax.dot_general(a, b, dims, preferred_element_type=f32)


def gates(x, r):
    z = x * r
    sig = 0.5 * jnp.tanh(0.5 * z) + 0.5
    act = z * sig
    slope = sig * (1.0 + z - act)
    return act, slope


def kernel(
    routes, codes, w_up, w_down, cot,
    out, grads, up_out, down_out,
    wu, wd, codes_all, cot_own, cot_all, table_v, table_s, place, stats,
    xbuf, up_acc, down_acc, inp3, cot3, yacc, move, land,
    up_v, down_v, ig_v, home_v,
    ssem, rsem, lsem,
):
    peers = lax.axis_size("peer")
    sections = lax.axis_size("section")
    slots = cot_own.shape[0]
    nblk = codes_all.shape[1]
    blk, width = codes_all.shape[2:]
    chunks, _, cols = wu.shape
    model = chunks * cols
    ring = peers // 2
    low, high = pl.ds(0, blk // 2), pl.ds(blk // 2, blk // 2)

    sec, me = lax.axis_index("section"), lax.axis_index("peer")
    nxt, prv = lax.rem(sec + 1, sections), lax.rem(sec + sections - 1, sections)
    xi, zi = me // 2, lax.rem(me, 2)
    zo = 1 - zi

    def at(dx, z):
        return 2 * lax.rem(xi + ring + dx, ring) + z

    zp, xr, xl, op = at(0, zo), at(1, zi), at(-1, zi), at(2, zi)
    xrz, xlz, opz = at(1, zo), at(-1, zo), at(2, zo)
    cross_out = lax.rem(sec, 2)
    cross_in = 1 - cross_out

    def crossed(p, cross):
        return p + cross * (1 - 2 * (p % 2 if isinstance(p, int) else lax.rem(p, 2)))

    there, sender = crossed(me, cross_out), crossed(me, cross_in)
    order = (me, zp, xl, xr, xlz, xrz, op, opz)

    barrier = pltpu.get_barrier_semaphore()
    for d in range(1, peers):
        pl.semaphore_signal(
            barrier, inc=1, device_id=(sec, lax.rem(me + d, peers)), device_id_type=MESH
        )
    for s in (nxt, prv):
        for p in range(peers):
            pl.semaphore_signal(barrier, inc=1, device_id=(s, p), device_id_type=MESH)

    def local(src, dst, i):
        c = pltpu.make_async_copy(src, dst, lsem.at[i])
        c.start()
        return c

    load_codes = local(codes, ig_v, slots + 1 + 2 * chunks)
    load_first = local(cot.at[pl.ds(0, blk)], cot_all.at[0, me], slots)
    load_cot = [local(cot.at[pl.ds(k * blk, blk)], cot_own.at[k], k) for k in range(slots)]
    load_up = [
        local(w_up.at[:, pl.ds(c * cols, cols)], wu.at[c], slots + 1 + c) for c in range(chunks)
    ]
    load_down = [
        local(w_down.at[pl.ds(c * cols, cols)], wd.at[c], slots + 1 + chunks + c)
        for c in range(chunks)
    ]
    r0, r1 = routes[0, 0], routes[0, 1]
    lane = lax.broadcasted_iota(jnp.int32, (8, 128), 1)
    table_v[peers] = jnp.where(lane == 0, r0, r1)

    def remote(src, dst, i, s, p):
        return pltpu.make_async_remote_copy(
            src_ref=src, dst_ref=dst, send_sem=ssem.at[i], recv_sem=rsem.at[i],
            device_id=(s, p), device_id_type=MESH,
        )

    sent = []

    def send(src, dst, i, s, p):
        c = remote(src, dst, i, s, p)
        c.start()
        sent.append(c)

    def arrived(dst, i):
        remote(dst, dst, i, sec, zp).wait_recv()

    FIRST, MORE = nblk, nblk + 1
    pieces = nblk + 2
    HOP = 7 * pieces
    ROUTE = HOP + nblk
    STAT = ROUTE + peers
    UPS = STAT + peers
    HOME = UPS + peers
    PACK = HOME + 1

    pl.semaphore_wait(barrier, 3 * peers - 1)

    def chunk(g, owner):
        if g < nblk:
            return codes_all.at[owner, g]
        return cot_all.at[g - nblk, owner]

    def pass_on(g, owner, o, p):
        send(chunk(g, owner), chunk(g, owner), 7 * g + o - 1, sec, p)

    def start_across(g):
        pass_on(g, me, 1, zp)

    def start_along(g):
        pass_on(g, me, 2, xr)
        pass_on(g, me, 3, xl)

    def wait_for(g, *numbers):
        for o in numbers:
            arrived(chunk(g, order[o]), 7 * g + o - 1)

    def pass_partner(g):
        wait_for(g, 1)
        pass_on(g, zp, 4, xr)
        pass_on(g, zp, 5, xl)

    def pass_opposite(g):
        if g % 2 == 0:
            wait_for(g, 2)
            pass_on(g, xl, 6, xr)
        else:
            wait_for(g, 3)
            pass_on(g, xr, 6, xl)

    def pass_across(g):
        wait_for(g, 6)
        pass_on(g, op, 7, zp)

    for d in range(peers):
        send(table_v.at[peers], table_v.at[me], ROUTE + d, nxt, lax.rem(me + d, peers))
    load_codes.wait()
    for b in range(nblk):
        send(ig_v.at[pl.ds(b * blk, blk)], codes_all.at[there, b], HOP + b, nxt, there)
    codes_sent = sent[-nblk:]
    del sent[-nblk:]
    load_first.wait()
    start_along(FIRST)

    for d in range(peers):
        j = lax.rem(me + d, peers)
        arrived(table_v.at[j], ROUTE + (peers - d) % peers)
    fetch = local(table_v, table_s, slots)
    fetch.wait()

    counts = [0] * peers
    slot_block, slot_live = [0] * slots, [0] * slots
    targets = []
    for p in range(peers):
        for b in range(nblk):
            q = table_s[p, 0, b]
            k = 0
            for n in range(peers):
                k = jnp.where(q == n, counts[n], k)
                counts[n] = counts[n] + jnp.where(q == n, 1, 0)
            for n in range(slots):
                here = (q == me) & (k == n)
                slot_block[n] = jnp.where(here, nblk * crossed(p, cross_in) + b, slot_block[n])
                slot_live[n] = jnp.where(here, 1, slot_live[n])
            targets.append((q, k))
    before = [0]
    for n in range(peers - 1):
        before.append(before[n] + counts[n] - 1)
    own_before = 0
    for n in range(peers):
        own_before = jnp.where(me == n, before[n], own_before)
    for n, (q, k) in enumerate(targets):
        ahead = 0
        for m in range(peers):
            ahead = jnp.where(q == m, before[m], ahead)
        place[n] = jnp.clip(jnp.where(k == 0, q, peers + ahead + k - 1), 0, 2 * peers - 1)

    for c in load_cot:
        c.wait()

    def mine(j):
        rows = jnp.zeros((blk, width), bf16)
        for k in range(1, slots):
            hit = (slot_live[k] == 1) & (own_before + k - 1 == j)
            rows = jnp.where(hit, cot_own[k], rows)
        return rows

    def pack_start():
        move[0] = mine(opz)
        send(move.at[0], land.at[0], PACK + 0, sec, zp)
        move[5] = mine(xrz)
        send(move.at[5], land.at[5], PACK + 5, sec, xr)
        move[6] = mine(xlz)
        send(move.at[6], land.at[6], PACK + 6, sec, xl)

    def pack_far():
        arrived(land.at[0], PACK + 0)
        move[1] = mine(op) + land[0]
        send(move.at[1, low], land.at[1, low], PACK + 1, sec, xr)
        send(move.at[1, high], land.at[1, high], PACK + 2, sec, xl)

    def pack_along():
        arrived(land.at[1, low], PACK + 1)
        arrived(land.at[1, high], PACK + 2)
        move[3] = mine(xr)
        move[3, low] = move[3, low] + land[1, low]
        send(move.at[3], land.at[3], PACK + 3, sec, xr)
        move[4] = mine(xl)
        move[4, high] = move[4, high] + land[1, high]
        send(move.at[4], land.at[4], PACK + 4, sec, xl)

    def pack_across():
        arrived(land.at[5], PACK + 5)
        arrived(land.at[6], PACK + 6)
        move[2] = mine(zp) + land[5] + land[6]
        send(move.at[2], land.at[2], PACK + 7, sec, zp)

    def pack_end():
        arrived(land.at[3], PACK + 3)
        arrived(land.at[4], PACK + 4)
        arrived(land.at[2], PACK + 7)
        cot_all[1, me] = mine(me) + land[3] + land[4] + land[2]

    def codes_here(g):
        arrived(codes_all.at[me, g], HOP + g)

    two = nblk * blk
    xs, ds = pl.ds(0, two), pl.ds(two, two)

    def x2_step(c, ssq):
        rows = jnp.concatenate([codes_all[me, b] for b in range(nblk)], axis=0)
        x = dot(rows, wu[c])
        xbuf[c, xs] = x
        return ssq + jnp.sum(x * x, axis=-1, keepdims=True)

    def slope_step(c, r):
        xbuf[c, ds] = gates(xbuf[c, xs], r)[1]
        return r

    pack_start()
    codes_here(0)
    start_along(0)
    start_across(0)
    pack_far()
    codes_here(1)
    start_along(1)
    for c in load_up:
        c.wait()
    ssq = lax.fori_loop(0, chunks, x2_step, jnp.zeros((two, 1), f32))
    r2 = lax.rsqrt(ssq * (1.0 / model) + eps)
    pack_along()
    pack_across()
    start_across(FIRST)
    pass_opposite(FIRST)
    start_across(1)
    lax.fori_loop(0, chunks, slope_step, r2)
    pack_end()
    start_along(MORE)
    start_across(MORE)
    pass_partner(FIRST)
    pass_across(FIRST)
    pass_opposite(MORE)
    pass_partner(MORE)
    pass_opposite(0)
    pass_opposite(1)
    pass_partner(0)
    pass_across(MORE)

    eye = lax.broadcasted_iota(jnp.int32, (blk, blk), 0) == lax.broadcasted_iota(
        jnp.int32, (blk, blk), 1
    )

    def as_row(col):
        return jnp.sum(jnp.where(eye, col, 0.0), axis=0, keepdims=True)

    def as_col(row):
        return jnp.sum(jnp.where(eye, row, 0.0), axis=1, keepdims=True)

    def cot_block(n):
        i = place[n]
        return cot_all[i // peers, lax.rem(i, peers)]

    for c in load_down:
        c.wait()
    wait_for(FIRST, 3, 4, 5, 7)
    wait_for(MORE, 2, 4, 5, 7)
    for b in range(nblk):
        cot3[pl.ds(b * blk, blk)] = cot_block(nblk * sender + b)

    def dz_step(c, m):
        dz = xbuf[c, ds] * dot(cot3[xs], wd[c], COLS_COLS)
        xbuf[c, ds] = dz
        return m + jnp.sum(xbuf[c, xs] * dz, axis=-1, keepdims=True)

    m2 = lax.fori_loop(0, chunks, dz_step, jnp.zeros((two, 1), f32), unroll=2) * (1.0 / model)
    c2 = (r2 * r2 * r2) * m2
    rows = [as_row(v[b * blk : (b + 1) * blk]) for v in (r2, c2) for b in range(nblk)]
    stats[me] = jnp.concatenate(rows + [jnp.zeros((8 - 2 * nblk, blk), f32)], axis=0)
    for d in range(1, peers):
        send(stats.at[me], stats.at[me], STAT + d, sec, lax.rem(me + d, peers))
    pass_partner(1)
    for g in range(nblk):
        pass_across(g)

    yacc[xs] = cot3[xs].astype(f32)

    def home_step(c, carry):
        dx = (r2 * xbuf[c, ds] - xbuf[c, xs] * c2).astype(bf16)
        yacc[xs] += dot(dx, wu[c], COLS_COLS)
        return carry

    lax.fori_loop(0, chunks, home_step, 0, unroll=2)
    for c in codes_sent:
        c.wait_send()
    ig_v[...] = yacc[xs].astype(bf16)
    send(ig_v, home_v, HOME, prv, sender)
    for d in range(1, peers):
        j = lax.rem(me + d, peers)
        arrived(stats.at[j], STAT + peers - d)

    up_acc[...] = jnp.zeros_like(up_acc)
    down_acc[...] = jnp.zeros_like(down_acc)

    def owner_of(o):
        q = order[0]
        for n in range(1, peers):
            q = jnp.where(o == n, order[n], q)
        return q

    def pair_step(i, carry):
        rs, cs = [], []
        for n in range(2):
            p = owner_of(2 * i + n)
            for b in range(nblk):
                part = pl.ds((nblk * n + b) * blk, blk)
                inp3[part] = codes_all[p, b]
                cot3[part] = cot_block(nblk * crossed(p, cross_in) + b)
            tile = stats[p]
            rs += [as_col(tile[b : b + 1]) for b in range(nblk)]
            cs += [as_col(tile[nblk + b : nblk + b + 1]) for b in range(nblk)]
        r, c3 = jnp.concatenate(rs, axis=0), jnp.concatenate(cs, axis=0)
        x = dot(inp3[...], wu[me])
        act, slope = gates(x, r)
        act = act.astype(bf16)
        back = dot(cot3[...], wd[me], COLS_COLS)
        dx = (r * (back * slope) - x * c3).astype(bf16)
        up_acc[...] += dot(inp3[...], dx, ROWS_ROWS)
        down_acc[...] += dot(act, cot3[...], ROWS_ROWS)
        return carry

    for g in range(nblk):
        wait_for(g, 3 if g % 2 == 0 else 2)
    lax.fori_loop(0, 2, pair_step, 0)
    for g in range(nblk):
        wait_for(g, 4, 5)
    lax.fori_loop(2, 3, pair_step, 0)
    for g in range(nblk):
        wait_for(g, 7)
    lax.fori_loop(3, peers // 2, pair_step, 0)

    saves = []
    factor = 1.0 / (peers * nblk)
    tall = width // peers
    up_v[...] = (up_acc[...] * factor).astype(bf16)
    for j in reversed(order[1:]):
        d = lax.rem(j + peers - me, peers)
        send(
            up_v.at[pl.ds(pl.multiple_of(j * tall, tall), tall)],
            up_out.at[:, pl.ds(pl.multiple_of(me * cols, cols), cols)],
            UPS + d, sec, j,
        )
    saves.append(local(
        up_v.at[pl.ds(pl.multiple_of(me * tall, tall), tall)],
        up_out.at[:, pl.ds(pl.multiple_of(me * cols, cols), cols)], 0,
    ))
    down_v[...] = (down_acc[...] * factor).astype(bf16)
    saves.append(local(down_v, down_out, 1))

    for k in range(slots):
        rows = codes_all[slot_block[k] // nblk, lax.rem(slot_block[k], nblk)]
        inp3[pl.ds(k * blk, blk)] = jnp.where(slot_live[k] == 1, rows, jnp.zeros_like(rows))

    def x_step(c, ssq):
        x = dot(inp3[...], wu[c])
        xbuf[c] = x
        return ssq + jnp.sum(x * x, axis=-1, keepdims=True)

    ssq = lax.fori_loop(0, chunks, x_step, jnp.zeros((slots * blk, 1), f32))
    r = lax.rsqrt(ssq * (1.0 / model) + eps)
    arrived(home_v, HOME)
    saves.append(local(home_v, grads, 2))
    yacc[...] = inp3[...].astype(f32)

    def y_step(c, carry):
        act, _ = gates(xbuf[c], r)
        yacc[...] += dot(act.astype(bf16), wd[c])
        return carry

    lax.fori_loop(0, chunks, y_step, 0)
    cot3[...] = yacc[...].astype(bf16)
    saves.append(local(cot3, out, 3))

    for d in range(1, peers):
        j = lax.rem(me + peers - d, peers)
        arrived(up_out.at[:, pl.ds(pl.multiple_of(j * cols, cols), cols)], UPS + d)
    for c in saves:
        c.wait()
    for c in sent:
        c.wait_send()


def copy_kernel(*refs):
    n = (len(refs) - 2) // 3
    sources, results, held = refs[:n], refs[n : 2 * n], refs[2 * n : 3 * n]
    in_sem, out_sem = refs[3 * n :]
    loads = []
    for src, mid in zip(sources, held):
        rows = src.shape[0] // 4
        for k in range(4):
            part = pl.ds(k * rows, rows)
            loads.append(pltpu.make_async_copy(src.at[part], mid.at[part], in_sem.at[len(loads)]))
    for c in loads:
        c.start()
    stores = []
    for mid, dst in zip(held, results):
        rows = dst.shape[0] // 4
        for k in range(4):
            part = pl.ds(k * rows, rows)
            loads[len(stores)].wait()
            c = pltpu.make_async_copy(mid.at[part], dst.at[part], out_sem.at[len(stores)])
            c.start()
            stores.append(c)
    for c in stores:
        c.wait()


def shards(codes, routes, w_up, w_down, cotangent):
    peers = lax.axis_size("peer")
    nblk = routes.shape[1]
    rows, width = codes.shape
    blk = rows // nblk
    slots = cotangent.shape[0] // blk
    model = w_up.shape[2]
    cols = model // peers
    anywhere = pl.BlockSpec(memory_space=pl.ANY)
    copies = 7 * (nblk + 2) + nblk + 2 + 3 * peers + 8
    shapes = (
        jax.ShapeDtypeStruct((slots * blk, width), bf16),
        jax.ShapeDtypeStruct((rows, width), bf16),
        jax.ShapeDtypeStruct((width // peers, model), bf16),
        jax.ShapeDtypeStruct((cols, width), bf16),
    )
    results = pl.pallas_call(
        kernel,
        out_shape=shapes,
        in_specs=[pl.BlockSpec(memory_space=pltpu.SMEM)] + [anywhere] * 4,
        out_specs=[anywhere] * 4,
        scratch_shapes=[
            pltpu.VMEM((peers, width, cols), bf16),
            pltpu.VMEM((peers, cols, width), bf16),
            pltpu.VMEM((peers, nblk, blk, width), bf16),
            pltpu.VMEM((slots, blk, width), bf16),
            pltpu.VMEM((2, peers, blk, width), bf16),
            pltpu.VMEM((peers + 1, 8, 128), jnp.int32),
            pltpu.SMEM((peers + 1, 8, 128), jnp.int32),
            pltpu.SMEM((2 * peers,), jnp.int32),
            pltpu.VMEM((peers, 8, blk), f32),
            pltpu.VMEM((peers, slots * blk, cols), f32),
            pltpu.VMEM((width, cols), f32),
            pltpu.VMEM((cols, width), f32),
            pltpu.VMEM((slots * blk, width), bf16),
            pltpu.VMEM((slots * blk, width), bf16),
            pltpu.VMEM((slots * blk, width), f32),
            pltpu.VMEM((7, blk, width), bf16),
            pltpu.VMEM((7, blk, width), bf16),
            pltpu.VMEM((width, cols), bf16),
            pltpu.VMEM((cols, width), bf16),
            pltpu.VMEM((rows, width), bf16),
            pltpu.VMEM((rows, width), bf16),
            pltpu.SemaphoreType.DMA((copies,)),
            pltpu.SemaphoreType.DMA((copies,)),
            pltpu.SemaphoreType.DMA((slots + 2 + 2 * peers,)),
        ],
        compiler_params=pltpu.CompilerParams(
            collective_id=0, has_side_effects=True, vmem_limit_bytes=62 * 1024 * 1024,
        ),
        name="relay",
    )(routes, codes, w_up[0], w_down[0], cotangent)
    out, grads, up, down = pl.pallas_call(
        copy_kernel,
        out_shape=shapes,
        in_specs=[anywhere] * 4,
        out_specs=[anywhere] * 4,
        scratch_shapes=[pltpu.VMEM(a.shape, a.dtype) for a in shapes]
        + [pltpu.SemaphoreType.DMA((16,))] * 2,
        name="results",
    )(*results)
    return out, grads, up[None], down[None]


def solution(mesh):
    placed = (
        P(("section", "peer"), None),
        P(("section", "peer"), None),
        P("section", None, None),
        P("section", None, None),
        P(("section", "peer"), None),
    )
    return jax.shard_map(
        shards,
        mesh=mesh,
        in_specs=placed,
        out_specs=(
            P(("section", "peer"), None),
            P(("section", "peer"), None),
            P("section", "peer", None),
            P("section", "peer", None),
        ),
        check_vma=False,
    )
```
